128 devices in a mesh: dp: 8 (over y, core), expert: 16 (over x, z).
Axes of the slice: x: 4, y: 4, z: 4, core: 2. Of those that a mesh axis runs over, the one named last changes fastest.
Arguments:
- tokens: bfloat16 [2048, 3072], P('expert', 'dp'), may hold values from -6 to 6
- grad_out: bfloat16 [2048, 3072], P('expert', 'dp'), may hold values from -0.59765625 to 0.59765625
- routes: int32 [2048, 4], P('expert'), may hold values from 0 to 15, all different within a row; in each aligned block of 128 rows (0 to 127, 128 to 255, ...) at most 48 rows name the same one
- gate_values: bfloat16 [2048, 4], P('expert'), may hold values from 0.099609375 to 1
- w_gate: bfloat16 [16, 5376, 3072], P('expert', 'dp'), may hold values from -0.109375 to 0.109375
- w_up: bfloat16 [16, 5376, 3072], P('expert', 'dp'), may hold values from -0.109375 to 0.109375
- w_down: bfloat16 [16, 5376, 3072], P('expert', 'dp'), may hold values from -0.078125 to 0.078125
Outputs:
- grad_tokens: bfloat16 [2048, 3072], P('expert', 'dp')
- grad_gates: float32 [2048, 4], P('expert')
- grad_w_gate: bfloat16 [16, 5376, 3072], P('expert', 'dp')
- grad_w_up: bfloat16 [16, 5376, 3072], P('expert', 'dp')
- grad_w_down: bfloat16 [16, 5376, 3072], P('expert', 'dp')
The draws below stay inside these ranges and needn't reach their ends.
Inputs may be any that keep to these rules, and one draw needn't show every extreme that they name: `routes`: the 4 experts of a token differ. Among the 128 tokens of one index of the expert axis (aligned blocks of tokens) no expert is chosen more than 48 times, and in every draw some expert is chosen exactly 48 times in some block.
All inputs are finite; a program needn't handle non-finite values.
Results may differ from the reference program's by a relative error of at most 0.011.
Values may be sent and summed in bfloat16 or wider, within the bound.
A program may use at most 128 MiB of HBM per device.

```python
import math
import jax
import jax.numpy as jnp
import numpy as np
from jax import lax

D = 3072
FF = 5376
TOPK = 4
TOK_DEV = 128
EXPERTS = 16
CAP = 48
TOKENS = 2048
N_EXPERT = 16


def level_of(key, extent, pieces, low, largest):
    level = 1.0
    for dim, shards_of in pieces:
        draws = jax.random.uniform(jax.random.fold_in(jax.random.fold_in(key, 6), dim), (shards_of,), jnp.float32, low / len(pieces), largest / len(pieces))
        level = level * jnp.repeat(jnp.exp(draws), extent[dim] // shards_of).reshape((-1,) + (1,) * (len(extent) - 1 - dim))
    return level


def shared_out(key, own, number, rows, count, top, reach, skew):
    sequence = jax.random.permutation(key, count)
    crowded, ordinary = portions_of(count, rows * top, reach, skew, True), portions_of(count, rows * top, reach, skew, False)
    places = jnp.arange(count)

    def named(tallies, rotation):
        used = int((tallies > 0).sum())
        fixed = max(1, used // 4)
        moved = fixed + (places - fixed + rotation * (used - fixed)) % max(1, count - fixed)
        return jnp.zeros((count,), jnp.int32).at[sequence[jnp.where(places < fixed, places, moved)]].set(jnp.asarray(tallies, jnp.int32))

    tallies = jnp.where(number % 4 == 0, named(crowded, number // 4), named(ordinary, number - number // 4 - 1))
    mixed = jax.random.permutation(jax.random.fold_in(own, 3), count)
    donor, taker = mixed[0:count // 2 * 2:2], mixed[1:count // 2 * 2:2]
    room = jnp.minimum(tallies[donor] - 1, reach - tallies[taker]) // 2
    room = jnp.where((donor == sequence[0]) | (taker == sequence[0]) | (tallies[taker] == 0), 0, jnp.maximum(room, 0))
    moved = jax.random.randint(jax.random.fold_in(own, 4), (count // 2,), 0, 1 << 20) % (room + 1)
    tallies = tallies.at[donor].add(-moved).at[taker].add(moved)
    labels = jnp.searchsorted(jnp.cumsum(tallies), jnp.arange(rows * top), side="right").astype(jnp.int32)
    table = labels.reshape(top, rows).T
    table = table[jax.random.permutation(jax.random.fold_in(own, 1), rows)]
    rotation = jax.random.randint(jax.random.fold_in(own, 2), (rows, 1), 0, top)
    return jnp.take_along_axis(table, (jnp.arange(top)[None, :] + rotation) % top, axis=1)


def portions_of(amount, total, most, slope, full):
    weights = [(1 << 20) // math.isqrt(standing ** slope) + 1 for standing in range(1, amount + 1)]
    largest = most if full else min(most, max(-(-total // amount), total * weights[0] // sum(weights)))
    least = 1 if total - largest >= amount - 1 else 0
    counts, spare = [largest] + [least] * (amount - 1), total - largest - least * (amount - 1)
    while spare > 0:
        candidates = [i for i in range(1, amount) if counts[i] < largest] or [i for i in range(1, amount) if counts[i] < most]
        whole, remaining = sum([weights[i] for i in candidates]), spare
        for i in candidates:
            extra = min(most - counts[i], max(1, remaining * weights[i] // whole), spare)
            counts[i] = counts[i] + extra
            spare = spare - extra
    return np.array(counts)


def scatter_about(rng, dims, width, most, split=(), kind=jnp.bfloat16):
    entries = width * jax.random.normal(rng, dims, jnp.float32)
    if split:
        entries = entries * level_of(rng, dims, split, -0.22, 0.18)
    return jnp.clip(entries, -most, most).astype(kind)


def setup_inputs(seed: int = 0) -> dict:
    key_of = jax.random.split(jax.random.key(seed), 8)
    tokens = scatter_about(key_of[0], (TOKENS, D), 1.0, 6.0, ((0, 16), (1, 8)))
    grad_out = scatter_about(key_of[1], (TOKENS, D), 0.1, 0.59765625, ((0, 16), (1, 8)))
    routes_keys = jax.random.split(jax.random.fold_in(key_of[2], 1), TOKENS // TOK_DEV)
    routes_turns = jax.random.permutation(jax.random.fold_in(key_of[2], 3), TOKENS // TOK_DEV)
    routes = jax.vmap(lambda own, number: shared_out(jax.random.fold_in(key_of[2], 2), own, number, TOK_DEV, EXPERTS, TOPK, CAP, 2))(routes_keys, routes_turns).reshape((TOKENS, TOPK))
    gate_values = jnp.clip(jnp.exp(math.log(1.0) - 2.306499 * jax.random.uniform(key_of[3], (TOKENS, TOPK), jnp.float32) ** level_of(key_of[3], (TOKENS, TOPK), ((0, 16),), -0.2, 0.2)), 0.099609375, 1.0).astype(jnp.bfloat16)
    w_gate = scatter_about(key_of[4], (EXPERTS, FF, D), D ** -0.5, 0.109375, ((0, 16), (1, 8)))
    w_up = scatter_about(key_of[5], (EXPERTS, FF, D), D ** -0.5, 0.109375, ((0, 16), (1, 8)))
    w_down = scatter_about(key_of[6], (EXPERTS, FF, D), FF ** -0.5, 0.078125, ((0, 16), (1, 8)))
    return dict(tokens=tokens, grad_out=grad_out, routes=routes, gate_values=gate_values, w_gate=w_gate, w_up=w_up, w_down=w_down)


def slot_index(block_routes, experts, capacity):
    flattened = block_routes.reshape(-1).astype(jnp.int32)
    onehot = (flattened[:, None] == jnp.arange(experts, dtype=jnp.int32)[None, :]).astype(jnp.int32)
    before = jnp.cumsum(onehot, axis=0) - onehot
    position = jnp.sum(before * onehot, axis=1)
    return (flattened * capacity + position).astype(jnp.int32)


def expert_backward(x_rows, dy_rows, gate_rows, weight_gate, weight_up, weight_down):
    pre_gate = jnp.dot(x_rows, weight_gate.T, preferred_element_type=jnp.float32)
    pre_up = jnp.dot(x_rows, weight_up.T, preferred_element_type=jnp.float32)
    projected = jnp.dot(dy_rows, weight_down.T, preferred_element_type=jnp.float32)
    squash = jax.nn.sigmoid(pre_gate)
    activated = pre_gate * squash
    hidden = (activated * pre_up).astype(jnp.bfloat16)
    gate_part = jnp.sum(projected * hidden.astype(jnp.float32), axis=1)
    scale = gate_rows.astype(jnp.float32)[:, None]
    hidden_grad = scale * projected
    d_gate = (hidden_grad * pre_up * squash * (1.0 + pre_gate * (1.0 - squash))).astype(jnp.bfloat16)
    d_up = (hidden_grad * activated).astype(jnp.bfloat16)
    d_out = (scale * dy_rows.astype(jnp.float32)).astype(jnp.bfloat16)
    input_part = jnp.dot(d_gate, weight_gate, preferred_element_type=jnp.float32) + jnp.dot(d_up, weight_up, preferred_element_type=jnp.float32)
    grad_gate_w = jnp.dot(d_gate.T, x_rows, preferred_element_type=jnp.float32).astype(jnp.bfloat16)
    grad_up_w = jnp.dot(d_up.T, x_rows, preferred_element_type=jnp.float32).astype(jnp.bfloat16)
    grad_down_w = jnp.dot(hidden.T, d_out, preferred_element_type=jnp.float32).astype(jnp.bfloat16)
    return input_part, gate_part, grad_gate_w, grad_up_w, grad_down_w


def reference(tokens, grad_out, routes, gate_values, w_gate, w_up, w_down):
    blocks = N_EXPERT
    pair_total = TOKENS * TOPK
    block_routes = routes.reshape(blocks, TOK_DEV, TOPK)

    def block_slots(part_routes):
        return slot_index(part_routes, EXPERTS, CAP)

    indices = jax.vmap(block_slots)(block_routes)
    expert_of = block_routes.reshape(blocks, TOK_DEV * TOPK).astype(jnp.int32)
    position = indices - expert_of * CAP
    destination = expert_of * (blocks * CAP) + jnp.arange(blocks, dtype=jnp.int32)[:, None] * CAP + position
    destination = destination.reshape(pair_total).astype(jnp.int32)
    token_of = (jnp.arange(pair_total, dtype=jnp.int32) // TOPK).astype(jnp.int32)
    slot_total = EXPERTS * blocks * CAP
    per_expert = blocks * CAP
    rows_x = jnp.zeros((slot_total, D), jnp.bfloat16).at[destination].set(tokens[token_of])
    rows_dy = jnp.zeros((slot_total, D), jnp.bfloat16).at[destination].set(grad_out[token_of])
    rows_gate = jnp.zeros((slot_total,), jnp.bfloat16).at[destination].set(gate_values.reshape(pair_total))

    def one_expert(packed):
        return expert_backward(packed[0], packed[1], packed[2], packed[3], packed[4], packed[5])

    results = lax.map(one_expert, (rows_x.reshape(EXPERTS, per_expert, D), rows_dy.reshape(EXPERTS, per_expert, D), rows_gate.reshape(EXPERTS, per_expert), w_gate, w_up, w_down))
    input_part, gate_part, grad_w_gate, grad_w_up, grad_w_down = results
    pair_grad = input_part.reshape(slot_total, D)[destination].reshape(TOKENS, TOPK, D)
    grad_tokens = jnp.sum(pair_grad, axis=1).astype(jnp.bfloat16)
    grad_gates = gate_part.reshape(slot_total)[destination].reshape(TOKENS, TOPK)
    return (grad_tokens, grad_gates, grad_w_gate, grad_w_up, grad_w_down)
```

```python
import jax
import jax.numpy as jnp
from jax import lax
from jax.experimental import pallas as pl
from jax.experimental.pallas import tpu as pltpu
from jax.sharding import PartitionSpec as P

MESH = pl.DeviceIdType.MESH
F32, BF16 = jnp.float32, jnp.bfloat16

TOK, D, FS, CAP, NB, TOPK = 128, 3072, 672, 48, 16, 4
DS = D // 8
SLOTS = NB * CAP
CH = 256
NCH = SLOTS // CH

REL = [
    (0, 0), (0, 1), (1, 0), (0, 3), (3, 0), (1, 1),
    (3, 3), (0, 2), (2, 0), (1, 3), (3, 1),
    (1, 2), (2, 1), (3, 2), (2, 3), (2, 2),
]
GROUPS = [(0, 6), (6, 11), (11, 16)]
RETURNS = [(0, 5), (5, 10), (10, 16)]


def split2(v):
    hi = v.astype(BF16)
    lo = (v - hi.astype(F32)).astype(BF16)
    return hi, lo


def nn(a, b):
    return lax.dot_general(a, b, (((1,), (0,)), ((), ())), preferred_element_type=F32)


def nt(a, b):
    return lax.dot_general(a, b, (((1,), (1,)), ((), ())), preferred_element_type=F32)


def tn(a, b):
    return lax.dot_general(a, b, (((0,), (0,)), ((), ())), preferred_element_type=F32)


class Sems:
    def __init__(self, send, recv):
        self.send, self.recv, self.names = send, recv, {}

    def index(self, name):
        return self.names.setdefault(name, len(self.names))


N_SEMS = 140


def main_kernel(
    tok_ref, dy_ref, routes_ref, gates_ref, wg_hbm, wu_hbm, wd_hbm,
    gtok_ref, ggate_ref, xdy_out, hg_out, dg_out, du_out,
    xdy, sel, pick, cols, wg, wu, wd, hg, dg, du, gsend, grecv, grow,
    gpart, gall, gback, ghome, dxf, dxb, sibr, rs_send, rs_recv, rows_back, home,
    send_sems, recv_sems, local_sems,
):
    dp, ex = lax.axis_index("dp"), lax.axis_index("expert")
    y, c = dp // 2, dp % 2
    x, z = ex // 4, ex % 4

    def dev(yy, cc, xx, zz):
        return (lax.rem(yy + 8, 4) * 2 + cc, lax.rem(xx + 8, 4) * 4 + lax.rem(zz + 8, 4))

    up, down, sib = dev(y + 1, c, x, z), dev(y - 1, c, x, z), dev(y, 1 - c, x, z)

    def toward(q):
        return dev(y, c, x - REL[q][0], z - REL[q][1])

    def origin(q):
        return dev(y, c, x + REL[q][0], z + REL[q][1])

    def peer(i):
        return (lax.rem(dp + i, 8), ex)

    sems = Sems(send_sems, recv_sems)
    sent = []

    def copy(name, src, dst, device):
        i = sems.index(name)
        return pltpu.make_async_remote_copy(
            src, dst, sems.send.at[i], sems.recv.at[i], device_id=device, device_id_type=MESH
        )

    def send(name, src, dst, device):
        cp = copy(name, src, dst, device)
        cp.start()
        sent.append(cp)

    def arrive(name, dst, device):
        copy(name, dst, dst, device).wait_recv()

    barrier = pltpu.get_barrier_semaphore()
    partners = [toward(q) for q in range(1, NB)] + [peer(i) for i in range(1, 8)]
    for p in partners:
        pl.semaphore_signal(barrier, inc=1, device_id=p, device_id_type=MESH)

    loads = []
    for i, (src, dst) in enumerate(((wg_hbm, wg), (wu_hbm, wu), (wd_hbm, wd))):
        cp = pltpu.make_async_copy(src.at[0], dst, local_sems.at[i])
        cp.start()
        loads.append(cp)

    r_i = lax.broadcasted_iota(jnp.int32, (TOK, TOK), 0)
    c_i = lax.broadcasted_iota(jnp.int32, (TOK, TOK), 1)
    eye = (r_i == c_i).astype(BF16)
    earlier = (r_i < c_i).astype(BF16)
    rt = tn(routes_ref[...].astype(F32).astype(BF16), eye).astype(jnp.int32)
    gt = tn(gates_ref[...], eye)
    code = ((x + 4 - rt // 4) % 4) * 4 + (z + 4 - rt % 4) % 4
    marks = [(code == a * 4 + b) for a, b in REL]
    count = jnp.concatenate([jnp.sum(m.astype(F32), axis=0, keepdims=True) for m in marks], axis=0)
    gate_of = jnp.concatenate(
        [jnp.sum(jnp.where(m, gt, 0.0), axis=0, keepdims=True) for m in marks], axis=0
    )
    place = nn(count.astype(BF16), earlier)
    place = jnp.where(count > 0, place, -1.0).astype(BF16)
    s_col = lax.broadcasted_iota(jnp.int32, (SLOTS, NB), 0)
    q_col = lax.broadcasted_iota(jnp.int32, (SLOTS, NB), 1)
    spread = ((s_col >= q_col * CAP) & (s_col < q_col * CAP + CAP)).astype(BF16)
    s_row = lax.broadcasted_iota(jnp.int32, (NB, SLOTS), 1)
    q_row = lax.broadcasted_iota(jnp.int32, (NB, SLOTS), 0)
    spread_t = (s_row >= q_row * CAP) & (s_row < q_row * CAP + CAP)
    s_full = lax.broadcasted_iota(jnp.int32, (SLOTS, TOK), 0).astype(F32)
    within = s_full - CAP * jnp.floor((s_full + 0.5) * (1.0 / CAP))
    lane = lax.broadcasted_iota(jnp.int32, (SLOTS, TOK), 1).astype(F32)
    cols[...] = (within == lane).astype(BF16)
    pick[...] = (nn(spread, place) == within).astype(BF16)
    sel[0] = nn(pick[...], tok_ref[...]).astype(BF16)
    sel[1] = nn(pick[...], dy_ref[...]).astype(BF16)
    gate_slots = jnp.where(spread_t, nt(gate_of.astype(BF16), pick[...]), 0.0)
    gate_slots = nn(gate_slots.astype(BF16), cols[...])
    for q in range(NB):
        gsend[q] = jnp.broadcast_to(gate_slots[q : q + 1], (8, TOK))

    pl.semaphore_wait(barrier, len(partners))

    def feat(yy):
        return pl.ds(pl.multiple_of((lax.rem(yy + 8, 4) * 2 + c) * DS, 128), DS)

    def feat_sib(yy):
        return pl.ds(pl.multiple_of((lax.rem(yy + 8, 4) * 2 + 1 - c) * DS, 128), DS)

    def block(q):
        return pl.ds(q * CAP, CAP)

    own0 = pltpu.make_async_copy(sel.at[:, block(0)], xdy.at[:, block(0), feat(y)], local_sems.at[3])
    own0.start()
    for q in range(1, NB):
        send(("x", q), sel.at[:, block(q)], xdy.at[:, block(q), feat(y)], toward(q))
    for q in range(1, NB):
        send(("g", q), gsend.at[q], grecv.at[q], toward(q))
    grecv[0] = gsend[0]

    def halves(g):
        a, b = GROUPS[g][0] * CAP, GROUPS[g][1] * CAP
        mid = a + (b - a + 31) // 32 * 16
        return pl.ds(a, b - a), pl.ds(a, mid - a), pl.ds(mid, b - mid)

    def gather_own(g):
        for q in range(*GROUPS[g]):
            if q == 0:
                own0.wait()
            else:
                arrive(("x", q), xdy.at[:, block(q), feat(y)], origin(q))
        full, _, _ = halves(g)
        mine = xdy.at[:, full, feat(y)]
        send(("up", g), mine, mine, up)
        send(("down", g), mine, mine, down)
        send(("sib", g), mine, mine, sib)

    def gather_relay(g):
        full, first, second = halves(g)
        below = xdy.at[:, full, feat(y - 1)]
        arrive(("up", g), below, down)
        part = xdy.at[:, first, feat(y - 1)]
        send(("up2", g), part, part, up)
        send(("sibb", g), below, below, sib)
        above = xdy.at[:, full, feat(y + 1)]
        arrive(("down", g), above, up)
        part = xdy.at[:, second, feat(y + 1)]
        send(("down2", g), part, part, down)
        send(("siba", g), above, above, sib)

    def gather_end(g):
        full, first, second = halves(g)
        far1, far2 = xdy.at[:, first, feat(y + 2)], xdy.at[:, second, feat(y + 2)]
        arrive(("up2", g), far1, down)
        send(("sib1", g), far1, far1, sib)
        arrive(("down2", g), far2, up)
        send(("sib2", g), far2, far2, sib)
        arrive(("sib", g), xdy.at[:, full, feat_sib(y)], sib)
        arrive(("sibb", g), xdy.at[:, full, feat_sib(y - 1)], sib)
        arrive(("siba", g), xdy.at[:, full, feat_sib(y + 1)], sib)
        arrive(("sib1", g), xdy.at[:, first, feat_sib(y + 2)], sib)
        arrive(("sib2", g), xdy.at[:, second, feat_sib(y + 2)], sib)

    stores = []

    def store(src, dst):
        cp = pltpu.make_async_copy(src, dst, local_sems.at[4 + len(stores)])
        cp.start()
        stores.append(cp)

    half = FS // 2

    def forward(j):
        rows = pl.ds(j * CH, CH)
        lanes = pl.ds(j * CH, CH)

        def step(i, total):
            units = pl.ds(pl.multiple_of(i * half, 16), half)
            pre_gate = nt(wg[units], xdy[0, rows])
            pre_up = nt(wu[units], xdy[0, rows])
            projected = nt(wd[units], xdy[1, rows])
            squash = jax.nn.sigmoid(pre_gate)
            activated = pre_gate * squash
            hidden = (activated * pre_up).astype(BF16).astype(F32)
            total = total + jnp.sum(projected * hidden, axis=0, keepdims=True)
            gates = grow[0:1, lanes]
            hg[units, lanes] = (hidden * gates).astype(BF16)
            grad = gates * projected
            dg[units, lanes] = (
                grad * pre_up * squash * (1.0 + pre_gate * (1.0 - squash))
            ).astype(BF16)
            du[units, lanes] = (grad * activated).astype(BF16)
            return total

        gpart[0:1, lanes] = lax.fori_loop(0, 2, step, jnp.zeros((1, CH), F32))
        store(xdy.at[:, rows], xdy_out.at[:, rows])

    def input_grad(j):
        lanes = pl.ds(j * CH, CH)
        for k in (2, 1, 3, 0):
            yy = lax.rem(y + k, 4)
            feats = pl.ds(pl.multiple_of(yy * 2 * DS, 128), 2 * DS)
            part = tn(dg[:, lanes], wg[:, feats]) + tn(du[:, lanes], wu[:, feats])
            dxf[j, 0, k] = part[:, :DS]
            dxf[j, 1, k] = part[:, DS:]
            dxb[j, k] = dxf[j, 1 - c, k].astype(BF16)
            send(("dx", j, k), dxb.at[j, k], sibr.at[j, k], sib)

    H = CH // 2

    def pair_sum(j, k, rows):
        return dxf[j, c, k, rows] + sibr[j, k, rows].astype(F32)

    lo, hi = pl.ds(0, H), pl.ds(H, H)

    def rs_hop(j, name, slot, value, device):
        rs_send[j, slot] = value.astype(BF16)
        send((name, j), rs_send.at[j, slot], rs_recv.at[j, slot], device)

    def scatter1(j):
        arrive(("dx", j, 2), sibr.at[j, 2], sib)
        rs_hop(j, "f_up", 0, pair_sum(j, 2, lo), up)
        rs_hop(j, "f_down", 1, pair_sum(j, 2, hi), down)
        arrive(("dx", j, 1), sibr.at[j, 1], sib)
        rs_hop(j, "d_up", 2, pair_sum(j, 1, hi), up)
        arrive(("dx", j, 3), sibr.at[j, 3], sib)
        rs_hop(j, "d_down", 3, pair_sum(j, 3, lo), down)

    def scatter2(j):
        arrive(("f_up", j), rs_recv.at[j, 0], down)
        rs_hop(j, "e_up", 4, pair_sum(j, 1, lo) + rs_recv[j, 0].astype(F32), up)
        arrive(("f_down", j), rs_recv.at[j, 1], up)
        rs_hop(j, "e_down", 5, pair_sum(j, 3, hi) + rs_recv[j, 1].astype(F32), down)

    def scatter3(j):
        arrive(("dx", j, 0), sibr.at[j, 0], sib)
        arrive(("d_up", j), rs_recv.at[j, 2], down)
        arrive(("d_down", j), rs_recv.at[j, 3], up)
        arrive(("e_up", j), rs_recv.at[j, 4], down)
        arrive(("e_down", j), rs_recv.at[j, 5], up)
        rows_back[pl.ds(j * CH, H)] = (
            pair_sum(j, 0, lo) + rs_recv[j, 4].astype(F32) + rs_recv[j, 3].astype(F32)
        ).astype(BF16)
        rows_back[pl.ds(j * CH + H, H)] = (
            pair_sum(j, 0, hi) + rs_recv[j, 2].astype(F32) + rs_recv[j, 5].astype(F32)
        ).astype(BF16)
        for q in range(*RETURNS[j]):
            if q > 0:
                send(("r", q), rows_back.at[block(q)], home.at[block(q)], origin(q))

    def gate_rows():
        for q in range(1, NB):
            arrive(("g", q), grecv.at[q], origin(q))
        table = jnp.concatenate([grecv[q, 0:1] for q in range(NB)], axis=0)
        wide = jnp.where(spread_t, nt(table.astype(BF16), cols[...]), 0.0)
        grow[...] = jnp.broadcast_to(jnp.sum(wide, axis=0, keepdims=True), (8, SLOTS))

    def gate_sums():
        wide = jnp.where(spread_t, jnp.broadcast_to(gpart[0:1], (NB, SLOTS)), 0.0)
        h, l = split2(wide)
        gall[dp] = nn(h, cols[...]) + nn(l, cols[...])
        for i in range(1, 8):
            send(("ga", i), gall.at[dp], gall.at[dp], peer(i))

    def gate_back():
        for i in range(1, 8):
            arrive(("ga", i), gall.at[lax.rem(dp + 8 - i, 8)], peer(8 - i))
        total = gall[0]
        for i in range(1, 8):
            total = total + gall[i]
        for q in range(NB):
            gback[q] = jnp.broadcast_to(total[q : q + 1], (8, TOK))
        for q in range(1, NB):
            send(("gr", q), gback.at[q], ghome.at[q], origin(q))
        ghome[0] = gback[0]

    def gate_end():
        for q in range(1, NB):
            arrive(("gr", q), ghome.at[q], toward(q))
        table = jnp.concatenate([ghome[q, 0:1] for q in range(NB)], axis=0)
        h, l = split2(table)
        wide = jnp.where(spread_t, nt(h, cols[...]) + nt(l, cols[...]), 0.0)
        h, l = split2(wide)
        per_token = nn(h, pick[...]) + nn(l, pick[...])
        out = jnp.zeros((TOPK, TOK), F32)
        for q in range(NB):
            out = out + jnp.where(marks[q], jnp.broadcast_to(per_token[q : q + 1], (TOPK, TOK)), 0.0)
        out = jnp.concatenate([out, jnp.zeros((8 - TOPK, TOK), F32)], axis=0)
        ggate_ref[...] = out.T[:, :TOPK]

    gather_own(0)
    gate_rows()
    gather_own(1)
    gather_relay(0)
    gather_own(2)
    for cp in loads:
        cp.wait()
    gather_end(0)
    gather_relay(1)
    forward(0)
    input_grad(0)
    gather_end(1)
    gather_relay(2)
    scatter1(0)
    forward(1)
    scatter2(0)
    input_grad(1)
    gather_end(2)
    scatter1(1)
    scatter3(0)
    forward(2)
    gate_sums()
    scatter2(1)
    input_grad(2)
    scatter1(2)
    scatter3(1)
    store(hg, hg_out)
    store(dg, dg_out)
    store(du, du_out)
    gate_back()
    scatter2(2)
    scatter3(2)
    home[block(0)] = rows_back[block(0)]
    gate_end()
    for q in range(1, NB):
        arrive(("r", q), home.at[block(q)], toward(q))
    gtok_ref[...] = tn(pick[...], home[...]).astype(BF16)
    for cp in sent:
        cp.wait_send()
    for cp in stores:
        cp.wait()


def exchange(tokens, grad_out, routes, gates, w_gate, w_up, w_down):
    vmem = pl.BlockSpec(memory_space=pltpu.VMEM)
    hbm = pl.BlockSpec(memory_space=pl.ANY)
    return pl.pallas_call(
        main_kernel,
        out_shape=(
            jax.ShapeDtypeStruct((TOK, DS), BF16),
            jax.ShapeDtypeStruct((TOK, TOPK), F32),
            jax.ShapeDtypeStruct((2, SLOTS, D), BF16),
            jax.ShapeDtypeStruct((FS, SLOTS), BF16),
            jax.ShapeDtypeStruct((FS, SLOTS), BF16),
            jax.ShapeDtypeStruct((FS, SLOTS), BF16),
        ),
        in_specs=[vmem] * 4 + [hbm] * 3,
        out_specs=(vmem, vmem, hbm, hbm, hbm, hbm),
        scratch_shapes=[
            pltpu.VMEM((2, SLOTS, D), BF16),
            pltpu.VMEM((2, SLOTS, DS), BF16),
            pltpu.VMEM((SLOTS, TOK), BF16),
            pltpu.VMEM((SLOTS, TOK), BF16),
            pltpu.VMEM((FS, D), BF16),
            pltpu.VMEM((FS, D), BF16),
            pltpu.VMEM((FS, D), BF16),
            pltpu.VMEM((FS, SLOTS), BF16),
            pltpu.VMEM((FS, SLOTS), BF16),
            pltpu.VMEM((FS, SLOTS), BF16),
            pltpu.VMEM((NB, 8, TOK), F32),
            pltpu.VMEM((NB, 8, TOK), F32),
            pltpu.VMEM((8, SLOTS), F32),
            pltpu.VMEM((8, SLOTS), F32),
            pltpu.VMEM((8, NB, TOK), F32),
            pltpu.VMEM((NB, 8, TOK), F32),
            pltpu.VMEM((NB, 8, TOK), F32),
            pltpu.VMEM((NCH, 2, 4, CH, DS), F32),
            pltpu.VMEM((NCH, 4, CH, DS), BF16),
            pltpu.VMEM((NCH, 4, CH, DS), BF16),
            pltpu.VMEM((NCH, 6, CH // 2, DS), BF16),
            pltpu.VMEM((NCH, 6, CH // 2, DS), BF16),
            pltpu.VMEM((SLOTS, DS), BF16),
            pltpu.VMEM((SLOTS, DS), BF16),
            pltpu.SemaphoreType.DMA((N_SEMS,)),
            pltpu.SemaphoreType.DMA((N_SEMS,)),
            pltpu.SemaphoreType.DMA((16,)),
        ],
        compiler_params=pltpu.CompilerParams(
            collective_id=0, has_side_effects=True, vmem_limit_bytes=60 << 20
        ),
        cost_estimate=pl.CostEstimate(
            flops=2 * 5 * SLOTS * FS * D, bytes_accessed=25_000_000, transcendentals=SLOTS * FS
        ),
    )(tokens, grad_out, routes, gates, w_gate, w_up, w_down)


def weight_kernel(xdy_ref, hg_ref, dg_ref, du_ref, og_ref, ou_ref, od_ref):
    og_ref[0] = nn(dg_ref[...], xdy_ref[0]).astype(BF16)
    ou_ref[0] = nn(du_ref[...], xdy_ref[0]).astype(BF16)
    od_ref[0] = nn(hg_ref[...], xdy_ref[1]).astype(BF16)


def weight_grads(xdy, hg, dg, du):
    tile = 512
    whole = pl.BlockSpec((FS, SLOTS), lambda i: (0, 0))
    out = pl.BlockSpec((1, FS, tile), lambda i: (0, 0, i))
    shape = jax.ShapeDtypeStruct((1, FS, D), BF16)
    return pl.pallas_call(
        weight_kernel,
        grid=(D // tile,),
        out_shape=(shape, shape, shape),
        in_specs=[pl.BlockSpec((2, SLOTS, tile), lambda i: (0, 0, i)), whole, whole, whole],
        out_specs=(out, out, out),
        compiler_params=pltpu.CompilerParams(vmem_limit_bytes=48 << 20),
        cost_estimate=pl.CostEstimate(
            flops=2 * 3 * SLOTS * FS * D, bytes_accessed=25_000_000, transcendentals=0
        ),
    )(xdy, hg, dg, du)


def per_device(tokens, grad_out, routes, gate_values, w_gate, w_up, w_down):
    grad_tokens, grad_gates, xdy, hg, dg, du = exchange(
        tokens, grad_out, routes, gate_values, w_gate, w_up, w_down
    )
    grad_w_gate, grad_w_up, grad_w_down = weight_grads(xdy, hg, dg, du)
    return grad_tokens, grad_gates, grad_w_gate, grad_w_up, grad_w_down


def solution(mesh):
    return jax.shard_map(
        per_device,
        mesh=mesh,
        in_specs=(
            P("expert", "dp"),
            P("expert", "dp"),
            P("expert", None),
            P("expert", None),
            P("expert", "dp", None),
            P("expert", "dp", None),
            P("expert", "dp", None),
        ),
        out_specs=(
            P("expert", "dp"),
            P("expert", None),
            P("expert", "dp", None),
            P("expert", "dp", None),
            P("expert", "dp", None),
        ),
        check_vma=False,
    )
```

```python
import jax
import jax.numpy as jnp
from jax import lax
from jax.experimental import pallas as pl
from jax.experimental.pallas import tpu as pltpu
from jax.sharding import PartitionSpec as P

MESH = pl.DeviceIdType.MESH
F32, BF16 = jnp.float32, jnp.bfloat16

TOK, D, FS, CAP, NB, TOPK = 128, 3072, 672, 48, 16, 4
DS = D // 8
SLOTS = NB * CAP
CH = 256
NCH = SLOTS // CH

REL = [
    (0, 0), (0, 1), (1, 0), (0, 3), (3, 0), (0, 2), (2, 0),
    (1, 1), (3, 3), (1, 3), (3, 1), (1, 2), (2, 1), (3, 2), (2, 3), (2, 2),
]
OWN = 0
GROUPS = [(7, 11), (11, 16)]
NEAR = (0, 7)
FAR_LIST = [*range(*GROUPS[0]), *range(*GROUPS[1])]
NEAR_LIST = [q for q in range(*NEAR) if q != OWN]
OTHERS = [*range(*GROUPS[0]), *NEAR_LIST, *range(*GROUPS[1])]
N0, NR = NEAR[0] * CAP, (NEAR[1] - NEAR[0]) * CAP
NEAR_ROWS = [(0, 256), (256, NR)]
NEAR_RETURNS = [(0, 5), (5, 7)]
RING_ROWS = [None, ((336, 96), (432, 80)), ((512, 128), (640, 128))]
FAR_RETURNS = [None, (7, 10), (10, 16)]


def split2(v):
    hi = v.astype(BF16)
    lo = (v - hi.astype(F32)).astype(BF16)
    return hi, lo


def nn(a, b):
    return lax.dot_general(a, b, (((1,), (0,)), ((), ())), preferred_element_type=F32)


def nt(a, b):
    return lax.dot_general(a, b, (((1,), (1,)), ((), ())), preferred_element_type=F32)


def tn(a, b):
    return lax.dot_general(a, b, (((0,), (0,)), ((), ())), preferred_element_type=F32)


class Sems:
    def __init__(self, send, recv):
        self.send, self.recv, self.names = send, recv, {}

    def index(self, name):
        return self.names.setdefault(name, len(self.names))


N_SEMS = 208


def main_kernel(
    tok_ref, dy_ref, routes_ref, gates_ref, wg_hbm, wu_hbm, wd_hbm,
    gtok_ref, ggate_ref, x_out, dg_out, du_out, down_out,
    xdy, raw, sel, selb, pick, cols, wg, wu, wd, act, slope, hid, hg, dg, du, stage, gsend, grecv, grow,
    gpart, gall, gback, ghome, dxf, dxb, sibr, rs_send, rs_recv, near_back, near_home,
    tsum, rows_back, home, send_sems, recv_sems, local_sems, load_sems, store_sems, stage_sems,
):
    dp, ex = lax.axis_index("dp"), lax.axis_index("expert")
    y, c = dp // 2, dp % 2
    x, z = ex // 4, ex % 4

    def dev(yy, cc, xx, zz):
        return (lax.rem(yy + 8, 4) * 2 + cc, lax.rem(xx + 8, 4) * 4 + lax.rem(zz + 8, 4))

    up, down, sib = dev(y + 1, c, x, z), dev(y - 1, c, x, z), dev(y, 1 - c, x, z)

    def toward(q):
        return dev(y, c, x - REL[q][0], z - REL[q][1])

    def origin(q):
        return dev(y, c, x + REL[q][0], z + REL[q][1])

    def peer(i):
        return (lax.rem(dp + i, 8), ex)

    sems = Sems(send_sems, recv_sems)
    sent = []

    def copy(name, src, dst, device):
        i = sems.index(name)
        return pltpu.make_async_remote_copy(
            src, dst, sems.send.at[i], sems.recv.at[i], device_id=device, device_id_type=MESH
        )

    def send(name, src, dst, device):
        cp = copy(name, src, dst, device)
        cp.start()
        sent.append(cp)

    def arrive(name, dst, device):
        copy(name, dst, dst, device).wait_recv()

    barrier = pltpu.get_barrier_semaphore()
    partners = [toward(q) for q in OTHERS] + [peer(i) for i in range(1, 8)]
    for p in partners:
        pl.semaphore_signal(barrier, inc=1, device_id=p, device_id_type=MESH)

    def stored(k, cc):
        return pl.ds(pl.multiple_of((lax.rem(y + k, 4) * 2 + cc) * DS, 128), DS)

    loads = []

    def load_weights():
        for i, (src, dst) in enumerate(((wg_hbm, wg), (wu_hbm, wu), (wd_hbm, wd))):
            for k in range(4):
                for cc in range(2):
                    cp = pltpu.make_async_copy(
                        src.at[0, :, stored(k, cc)],
                        dst.at[:, pl.ds((cc * 4 + k) * DS, DS)],
                        load_sems.at[i * 8 + k * 2 + cc],
                    )
                    cp.start()
                    loads.append(cp)

    def feat(k):
        return pl.ds(pl.multiple_of((c * 4 + k) * DS, 128), DS)

    def feat_sib(k):
        return pl.ds(pl.multiple_of(((1 - c) * 4 + k) * DS, 128), DS)

    def block(q):
        return pl.ds(q * CAP, CAP)

    T1, T2 = pl.ds(0, TOK // 2), pl.ds(TOK // 2, TOK // 2)
    raw[0, 0] = tok_ref[...]
    raw[0, 1] = dy_ref[...]

    r_i = lax.broadcasted_iota(jnp.int32, (TOK, TOK), 0)
    c_i = lax.broadcasted_iota(jnp.int32, (TOK, TOK), 1)
    earlier = (r_i < c_i).astype(BF16)
    rt = routes_ref[...]
    gt = gates_ref[...].astype(F32)
    code = ((x + 4 - rt // 4) % 4) * 4 + (z + 4 - rt % 4) % 4
    marks = [(code == a * 4 + b) for a, b in REL]
    count = jnp.concatenate([jnp.sum(m.astype(F32), axis=0, keepdims=True) for m in marks], axis=0)
    gate_of = jnp.concatenate(
        [jnp.sum(jnp.where(m, gt, 0.0), axis=0, keepdims=True) for m in marks], axis=0
    )
    place = nn(count.astype(BF16), earlier)
    place = jnp.where(count > 0, place, -1.0).astype(BF16)
    s_col = lax.broadcasted_iota(jnp.int32, (SLOTS, NB), 0)
    q_col = lax.broadcasted_iota(jnp.int32, (SLOTS, NB), 1)
    spread = ((s_col >= q_col * CAP) & (s_col < q_col * CAP + CAP)).astype(BF16)
    s_row = lax.broadcasted_iota(jnp.int32, (NB, SLOTS), 1)
    q_row = lax.broadcasted_iota(jnp.int32, (NB, SLOTS), 0)
    spread_t = (s_row >= q_row * CAP) & (s_row < q_row * CAP + CAP)
    s_full = lax.broadcasted_iota(jnp.int32, (SLOTS, TOK), 0).astype(F32)
    within = s_full - CAP * jnp.floor((s_full + 0.5) * (1.0 / CAP))
    lane = lax.broadcasted_iota(jnp.int32, (SLOTS, TOK), 1).astype(F32)
    pick[...] = (nn(spread, place) == within).astype(BF16)

    def raw_send(a):
        send(("raw_up", a), raw.at[0, a], raw.at[3, a], up)
        send(("raw_down", a), raw.at[0, a], raw.at[1, a], down)

    def select(a):
        sel[a] = nn(pick[...], raw[0, a]).astype(BF16)

    own = {}

    def own_block(src, a, k):
        cp = pltpu.make_async_copy(src, xdy.at[a, block(OWN), feat(k)], local_sems.at[a * 4 + k])
        cp.start()
        own[a, k] = cp

    def rows_send(a, blocks):
        for q in blocks:
            if q == OWN:
                own_block(sel.at[a, block(OWN)], a, 0)
            else:
                send(("x", q, a), sel.at[a, block(q)], xdy.at[a, block(q), feat(0)], toward(q))

    def gates_send():
        cols[...] = (within == lane).astype(BF16)
        gate_slots = jnp.where(spread_t, nt(gate_of.astype(BF16), pick[...]), 0.0)
        gate_slots = nn(gate_slots.astype(BF16), cols[...])
        for q in range(NB):
            gsend[q] = jnp.broadcast_to(gate_slots[q : q + 1], (8, TOK))
        for q in OTHERS:
            send(("g", q), gsend.at[q], grecv.at[q], toward(q))
        grecv[OWN] = gsend[OWN]

    near = pl.ds(N0, NR)

    def near_send(a, k):
        selb[k - 1, a] = nn(pick[near], raw[k, a]).astype(BF16)
        for q in NEAR_LIST:
            src = selb.at[k - 1, a, pl.ds(q * CAP - N0, CAP)]
            send(("n", q, k, a), src, xdy.at[a, block(q), feat(k)], toward(q))
        own_block(selb.at[k - 1, a, pl.ds(OWN * CAP - N0, CAP)], a, k)

    def raw_relay(a):
        arrive(("raw_up", a), raw.at[3, a], down)
        send(("raw_up2", a), raw.at[3, a, T1], raw.at[2, a, T1], up)
        arrive(("raw_down", a), raw.at[1, a], up)
        send(("raw_down2", a), raw.at[1, a, T2], raw.at[2, a, T2], down)

    def raw_end(a):
        arrive(("raw_up2", a), raw.at[2, a, T1], down)
        arrive(("raw_down2", a), raw.at[2, a, T2], up)

    def near_share(a, k):
        own[a, k].wait()
        for q in NEAR_LIST:
            name = ("x", q, a) if k == 0 else ("n", q, k, a)
            arrive(name, xdy.at[a, block(q), feat(k)], origin(q))
        mine = xdy.at[a, near, feat(k)]
        send(("nsib", k, a), mine, mine, sib)

    def near_end(a):
        for k in range(4):
            arrive(("nsib", k, a), xdy.at[a, near, feat_sib(k)], sib)

    def halves(g):
        a, b = GROUPS[g][0] * CAP, GROUPS[g][1] * CAP
        mid = a + (b - a + 31) // 32 * 16
        return pl.ds(a, b - a), pl.ds(a, mid - a), pl.ds(mid, b - mid)

    def gather_own(g, a):
        for q in range(*GROUPS[g]):
            arrive(("x", q, a), xdy.at[a, block(q), feat(0)], origin(q))
        full, _, _ = halves(g)
        mine = xdy.at[a, full, feat(0)]
        send(("up", g, a), mine, xdy.at[a, full, feat(3)], up)
        send(("down", g, a), mine, xdy.at[a, full, feat(1)], down)
        send(("sib", g, a), mine, mine, sib)

    def gather_relay(g, a):
        full, first, second = halves(g)
        below = xdy.at[a, full, feat(3)]
        arrive(("up", g, a), below, down)
        send(("up2", g, a), xdy.at[a, first, feat(3)], xdy.at[a, first, feat(2)], up)
        above = xdy.at[a, full, feat(1)]
        arrive(("down", g, a), above, up)
        send(("down2", g, a), xdy.at[a, second, feat(1)], xdy.at[a, second, feat(2)], down)
        send(("sibb", g, a), below, below, sib)
        send(("siba", g, a), above, above, sib)

    def gather_end(g, a):
        full, first, second = halves(g)
        far1, far2 = xdy.at[a, first, feat(2)], xdy.at[a, second, feat(2)]
        arrive(("up2", g, a), far1, down)
        send(("sib1", g, a), far1, far1, sib)
        arrive(("down2", g, a), far2, up)
        send(("sib2", g, a), far2, far2, sib)
        arrive(("sib", g, a), xdy.at[a, full, feat_sib(0)], sib)
        arrive(("sibb", g, a), xdy.at[a, full, feat_sib(3)], sib)
        arrive(("siba", g, a), xdy.at[a, full, feat_sib(1)], sib)
        arrive(("sib1", g, a), xdy.at[a, first, feat_sib(2)], sib)
        arrive(("sib2", g, a), xdy.at[a, second, feat_sib(2)], sib)

    stores = []

    def store(src, dst):
        cp = pltpu.make_async_copy(src, dst, store_sems.at[len(stores)])
        cp.start()
        stores.append(cp)

    half = FS // 2

    def gate_up(j):
        rows = pl.ds(j * CH, CH)

        def step(i, carry):
            units = pl.ds(pl.multiple_of(i * half, 16), half)
            pre_gate = nt(wg[units], xdy[0, rows])
            pre_up = nt(wu[units], xdy[0, rows])
            squash = jax.nn.sigmoid(pre_gate)
            activated = pre_gate * squash
            hid[units, rows] = (activated * pre_up).astype(BF16)
            act[j, units] = activated
            slope[j, units] = pre_up * squash * (1.0 + pre_gate * (1.0 - squash))
            return carry

        lax.fori_loop(0, 2, step, 0)
        for k in range(4):
            for cc in range(2):
                src = xdy.at[0, rows, pl.ds((cc * 4 + k) * DS, DS)]
                store(src, x_out.at[rows, stored(k, cc)])

    def hidden_grad(j):
        rows = pl.ds(j * CH, CH)

        def step(i, total):
            units = pl.ds(pl.multiple_of(i * half, 16), half)
            projected = nt(wd[units], xdy[1, rows])
            hidden = hid[units, rows].astype(F32)
            gates = grow[0:1, rows]
            hg[units, rows] = (hidden * gates).astype(BF16)
            grad = gates * projected
            dg[units, rows] = (grad * slope[j, units]).astype(BF16)
            du[units, rows] = (grad * act[j, units]).astype(BF16)
            return total + jnp.sum(projected * hidden, axis=0, keepdims=True)

        gpart[0:1, rows] = lax.fori_loop(0, 2, step, jnp.zeros((1, CH), F32))

    def input_grad(j, ks=(2, 0)):
        rows = pl.ds(j * CH, CH)
        for k in ks:
            for core in (1 - c, c):
                feats = pl.ds(pl.multiple_of((core * 4 + k) * DS, 128), 2 * DS)
                part = tn(dg[:, rows], wg[:, feats]) + tn(du[:, rows], wu[:, feats])
                if core is c:
                    dxf[k, rows] = part[:, :DS]
                    dxf[k + 1, rows] = part[:, DS:]
                else:
                    dxb[k, rows] = part[:, :DS].astype(BF16)
                    dxb[k + 1, rows] = part[:, DS:].astype(BF16)
                    pair = pl.ds(k, 2)
                    send(("dx", j, k), dxb.at[pair, rows], sibr.at[pair, rows], sib)

    def dx_arrive(j, k):
        arrive(("dx", j, k), sibr.at[pl.ds(k, 2), pl.ds(j * CH, CH)], sib)

    def pair_sum(k, rows):
        return dxf[k, rows] + sibr[k, rows].astype(F32)

    pieces = []

    def down_piece(i):
        if i >= 2:
            for cp in pieces[2 * (i - 2) : 2 * (i - 1)]:
                cp.wait()
        cc, k = i // 2, i % 2 * 2
        stage[i % 2] = nn(hg[...], xdy[1, :, pl.ds((cc * 4 + k) * DS, 2 * DS)]).astype(BF16)
        for m in range(2):
            cp = pltpu.make_async_copy(
                stage.at[i % 2, :, pl.ds(m * DS, DS)],
                down_out.at[:, stored(k + m, cc)],
                stage_sems.at[i * 2 + m],
            )
            cp.start()
            pieces.append(cp)

    class RingSum:
        def __init__(self, i, part, first, second):
            self.i, self.part, self.first, self.second = i, part, pl.ds(*first), pl.ds(*second)

        def buffer(self, ref, slot, rows):
            return ref.at[self.i, slot, pl.ds(0, rows.size)]

        def hop(self, name, slot, value, rows, device):
            src = self.buffer(rs_send, slot, rows)
            src[...] = value.astype(BF16)
            send((name, self.i), src, self.buffer(rs_recv, slot, rows), device)

        def take(self, name, slot, rows, device):
            dst = self.buffer(rs_recv, slot, rows)
            arrive((name, self.i), dst, device)
            return dst[...].astype(F32)

        def far(self):
            self.hop("f_up", 0, self.part(2, self.first), self.first, up)
            self.hop("f_down", 1, self.part(2, self.second), self.second, down)
            self.hop("d_down", 3, self.part(3, self.first), self.first, down)

        def near(self):
            self.hop("d_up", 2, self.part(1, self.second), self.second, up)

        def relay(self):
            got = self.take("f_up", 0, self.first, down)
            self.hop("e_up", 4, self.part(1, self.first) + got, self.first, up)
            got = self.take("f_down", 1, self.second, up)
            self.hop("e_down", 5, self.part(3, self.second) + got, self.second, down)

        def sums(self):
            a = self.part(0, self.first) + self.take("d_down", 3, self.first, up)
            a = a + self.take("e_up", 4, self.first, down)
            b = self.part(0, self.second) + self.take("d_up", 2, self.second, down)
            b = b + self.take("e_down", 5, self.second, up)
            return a, b

    rings = [r and RingSum(j, pair_sum, *r) for j, r in enumerate(RING_ROWS)]

    def scatter1(j):
        dx_arrive(j, 2)
        rings[j].far()
        dx_arrive(j, 0)
        rings[j].near()

    def scatter3(j):
        for value, rows in zip(rings[j].sums(), RING_ROWS[j]):
            rows_back[pl.ds(*rows)] = value.astype(BF16)
        for q in range(*FAR_RETURNS[j]):
            send(("r", q), rows_back.at[block(q)], home.at[block(q)], origin(q))

    def near_return(j):
        a, b = NEAR_ROWS[j]
        for k in range(4):
            near_back[k, pl.ds(a - N0, b - a)] = pair_sum(k, pl.ds(a, b - a)).astype(BF16)
        for q in range(*NEAR_RETURNS[j]):
            rows = pl.ds(q * CAP - N0, CAP)
            if q == OWN:
                near_home[:, rows] = near_back[:, rows]
            else:
                send(("nr", q), near_back.at[:, rows], near_home.at[:, rows], origin(q))

    def near_combine():
        for q in NEAR_LIST:
            arrive(("nr", q), near_home.at[:, pl.ds(q * CAP - N0, CAP)], toward(q))
        for k in (2, 1, 3, 0):
            tsum[k] = tn(pick[near], near_home[k])

    token_ring = RingSum(0, lambda k, rows: tsum[k, rows], (0, TOK // 2), (TOK // 2, TOK // 2))

    def gate_rows():
        for q in OTHERS:
            arrive(("g", q), grecv.at[q], origin(q))
        table = jnp.concatenate([grecv[q, 0:1] for q in range(NB)], axis=0)
        wide = jnp.where(spread_t, nt(table.astype(BF16), cols[...]), 0.0)
        grow[...] = jnp.broadcast_to(jnp.sum(wide, axis=0, keepdims=True), (8, SLOTS))

    def gate_sums():
        wide = jnp.where(spread_t, jnp.broadcast_to(gpart[0:1], (NB, SLOTS)), 0.0)
        h, l = split2(wide)
        gall[dp] = nn(h, cols[...]) + nn(l, cols[...])
        for i in range(1, 8):
            send(("ga", i), gall.at[dp], gall.at[dp], peer(i))

    def gate_back():
        for i in range(1, 8):
            arrive(("ga", i), gall.at[lax.rem(dp + 8 - i, 8)], peer(8 - i))
        total = gall[0]
        for i in range(1, 8):
            total = total + gall[i]
        for q in range(NB):
            gback[q] = jnp.broadcast_to(total[q : q + 1], (8, TOK))
        for q in OTHERS:
            send(("gr", q), gback.at[q], ghome.at[q], origin(q))
        ghome[OWN] = gback[OWN]

    def gate_end():
        for q in OTHERS:
            arrive(("gr", q), ghome.at[q], toward(q))
        table = jnp.concatenate([ghome[q, 0:1] for q in range(NB)], axis=0)
        h, l = split2(table)
        wide = jnp.where(spread_t, nt(h, cols[...]) + nt(l, cols[...]), 0.0)
        h, l = split2(wide)
        per_token = nn(h, pick[...]) + nn(l, pick[...])
        out = jnp.zeros((TOPK, TOK), F32)
        for q in range(NB):
            out = out + jnp.where(marks[q], jnp.broadcast_to(per_token[q : q + 1], (TOPK, TOK)), 0.0)
        ggate_ref[...] = out

    far0, far1, close = range(*GROUPS[0]), range(*GROUPS[1]), range(*NEAR)
    select(0)
    pl.semaphore_wait(barrier, len(partners))
    raw_send(0)
    rows_send(0, far0)
    rows_send(0, close)
    raw_send(1)
    rows_send(0, far1)
    select(1)
    load_weights()
    raw_relay(0)
    near_send(0, 3)
    near_send(0, 1)
    gather_own(0, 0)
    raw_relay(1)
    raw_end(0)
    near_send(0, 2)
    rows_send(1, far0)
    rows_send(1, close)
    gather_own(1, 0)
    near_send(1, 3)
    near_send(1, 1)
    gates_send()
    near_share(0, 0)
    rows_send(1, far1)
    raw_end(1)
    near_send(1, 2)
    gather_relay(0, 0)
    near_share(0, 3)
    near_share(0, 1)
    near_share(0, 2)
    near_end(0)
    for cp in loads:
        cp.wait()
    gather_own(0, 1)
    gate_up(0)
    gather_relay(1, 0)
    near_share(1, 0)
    gather_end(0, 0)
    gate_up(1)
    gather_relay(0, 1)
    gather_end(1, 0)
    near_share(1, 3)
    near_share(1, 1)
    gate_up(2)
    gate_rows()
    gather_own(1, 1)
    near_share(1, 2)
    near_end(1)
    hidden_grad(0)
    input_grad(0)
    gather_relay(1, 1)
    gather_end(0, 1)
    hidden_grad(1)
    dx_arrive(0, 2)
    dx_arrive(0, 0)
    near_return(0)
    input_grad(1)
    gather_end(1, 1)
    hidden_grad(2)
    dx_arrive(1, 2)
    rings[1].far()
    dx_arrive(1, 0)
    rings[1].near()
    near_return(1)
    input_grad(2, (2,))
    rings[1].relay()
    input_grad(2, (0,))
    dx_arrive(2, 2)
    rings[2].far()
    dx_arrive(2, 0)
    rings[2].near()
    gate_sums()
    store(dg, dg_out)
    store(du, du_out)
    scatter3(1)
    near_combine()
    down_piece(0)
    rings[2].relay()
    token_ring.far()
    token_ring.near()
    gate_back()
    down_piece(1)
    scatter3(2)
    token_ring.relay()
    down_piece(2)
    gate_end()
    down_piece(3)
    first, second = token_ring.sums()
    for q in FAR_LIST:
        arrive(("r", q), home.at[block(q)], toward(q))
    far_sum = jnp.zeros((TOK, DS), F32)
    for a, b in GROUPS:
        rows = pl.ds(a * CAP, (b - a) * CAP)
        far_sum = far_sum + tn(pick[rows], home[rows])
    gtok_ref[T1] = (far_sum[: TOK // 2] + first).astype(BF16)
    gtok_ref[T2] = (far_sum[TOK // 2 :] + second).astype(BF16)
    for cp in pieces[4:]:
        cp.wait()
    for cp in sent:
        cp.wait_send()
    for cp in stores:
        cp.wait()


def exchange(tokens, grad_out, routes, gates, w_gate, w_up, w_down):
    vmem = pl.BlockSpec(memory_space=pltpu.VMEM)
    hbm = pl.BlockSpec(memory_space=pl.ANY)
    return pl.pallas_call(
        main_kernel,
        out_shape=(
            jax.ShapeDtypeStruct((TOK, DS), BF16),
            jax.ShapeDtypeStruct((TOPK, TOK), F32),
            jax.ShapeDtypeStruct((SLOTS, D), BF16),
            jax.ShapeDtypeStruct((FS, SLOTS), BF16),
            jax.ShapeDtypeStruct((FS, SLOTS), BF16),
            jax.ShapeDtypeStruct((FS, D), BF16),
        ),
        in_specs=[vmem] * 4 + [hbm] * 3,
        out_specs=(vmem, vmem, hbm, hbm, hbm, hbm),
        scratch_shapes=[
            pltpu.VMEM((2, SLOTS, D), BF16),
            pltpu.VMEM((4, 2, TOK, DS), BF16),
            pltpu.VMEM((2, SLOTS, DS), BF16),
            pltpu.VMEM((3, 2, NR, DS), BF16),
            pltpu.VMEM((SLOTS, TOK), BF16),
            pltpu.VMEM((SLOTS, TOK), BF16),
            pltpu.VMEM((FS, D), BF16),
            pltpu.VMEM((FS, D), BF16),
            pltpu.VMEM((FS, D), BF16),
            pltpu.VMEM((NCH, FS, CH), F32),
            pltpu.VMEM((NCH, FS, CH), F32),
            pltpu.VMEM((FS, SLOTS), BF16),
            pltpu.VMEM((FS, SLOTS), BF16),
            pltpu.VMEM((FS, SLOTS), BF16),
            pltpu.VMEM((FS, SLOTS), BF16),
            pltpu.VMEM((2, FS, 2 * DS), BF16),
            pltpu.VMEM((NB, 8, TOK), F32),
            pltpu.VMEM((NB, 8, TOK), F32),
            pltpu.VMEM((8, SLOTS), F32),
            pltpu.VMEM((8, SLOTS), F32),
            pltpu.VMEM((8, NB, TOK), F32),
            pltpu.VMEM((NB, 8, TOK), F32),
            pltpu.VMEM((NB, 8, TOK), F32),
            pltpu.VMEM((4, SLOTS, DS), F32),
            pltpu.VMEM((4, SLOTS, DS), BF16),
            pltpu.VMEM((4, SLOTS, DS), BF16),
            pltpu.VMEM((3, 6, CH // 2, DS), BF16),
            pltpu.VMEM((3, 6, CH // 2, DS), BF16),
            pltpu.VMEM((4, NR, DS), BF16),
            pltpu.VMEM((4, NR, DS), BF16),
            pltpu.VMEM((4, TOK, DS), F32),
            pltpu.VMEM((SLOTS, DS), BF16),
            pltpu.VMEM((SLOTS, DS), BF16),
            pltpu.SemaphoreType.DMA((N_SEMS,)),
            pltpu.SemaphoreType.DMA((N_SEMS,)),
            pltpu.SemaphoreType.DMA((8,)),
            pltpu.SemaphoreType.DMA((24,)),
            pltpu.SemaphoreType.DMA((26,)),
            pltpu.SemaphoreType.DMA((8,)),
        ],
        compiler_params=pltpu.CompilerParams(
            collective_id=0, has_side_effects=True, vmem_limit_bytes=60 << 20
        ),
        cost_estimate=pl.CostEstimate(
            flops=2 * 5 * SLOTS * FS * D, bytes_accessed=25_000_000, transcendentals=SLOTS * FS
        ),
    )(tokens, grad_out, routes.T, gates.T, w_gate, w_up, w_down)


def weight_kernel(
    tok_ref, gate_ref, x_ref, dg_ref, du_ref, down_ref, tok_out, gate_out, og_ref, ou_ref, od_ref
):
    @pl.when(pl.program_id(0) == 0)
    def _():
        tok_out[...] = tok_ref[...]
        gate_out[...] = gate_ref[...]

    og_ref[0] = nn(dg_ref[...], x_ref[...]).astype(BF16)
    ou_ref[0] = nn(du_ref[...], x_ref[...]).astype(BF16)
    od_ref[0] = down_ref[...]


def weight_grads(grad_tokens, grad_gates, x, dg, du, down):
    tile = 512
    whole = pl.BlockSpec((FS, SLOTS), lambda i: (0, 0))
    small = [pl.BlockSpec(a.shape, lambda i: (0, 0)) for a in (grad_tokens, grad_gates)]
    out = pl.BlockSpec((1, FS, tile), lambda i: (0, 0, i))
    shape = jax.ShapeDtypeStruct((1, FS, D), BF16)
    return pl.pallas_call(
        weight_kernel,
        grid=(D // tile,),
        out_shape=(
            jax.ShapeDtypeStruct(grad_tokens.shape, BF16),
            jax.ShapeDtypeStruct(grad_gates.shape, F32),
            shape, shape, shape,
        ),
        in_specs=[
            *small,
            pl.BlockSpec((SLOTS, tile), lambda i: (0, i)),
            whole,
            whole,
            pl.BlockSpec((FS, tile), lambda i: (0, i)),
        ],
        out_specs=(*small, out, out, out),
        compiler_params=pltpu.CompilerParams(vmem_limit_bytes=62 << 20),
        cost_estimate=pl.CostEstimate(
            flops=2 * 2 * SLOTS * FS * D, bytes_accessed=25_000_000, transcendentals=0
        ),
    )(grad_tokens, grad_gates, x, dg, du, down)


def per_device(tokens, grad_out, routes, gate_values, w_gate, w_up, w_down):
    grad_tokens, grad_gates, x, dg, du, down = exchange(
        tokens, grad_out, routes, gate_values, w_gate, w_up, w_down
    )
    grad_tokens, grad_gates, grad_w_gate, grad_w_up, grad_w_down = weight_grads(
        grad_tokens, grad_gates, x, dg, du, down
    )
    return grad_tokens, grad_gates.T, grad_w_gate, grad_w_up, grad_w_down


def solution(mesh):
    return jax.shard_map(
        per_device,
        mesh=mesh,
        in_specs=(
            P("expert", "dp"),
            P("expert", "dp"),
            P("expert", None),
            P("expert", None),
            P("expert", "dp", None),
            P("expert", "dp", None),
            P("expert", "dp", None),
        ),
        out_specs=(
            P("expert", "dp"),
            P("expert", None),
            P("expert", "dp", None),
            P("expert", "dp", None),
            P("expert", "dp", None),
        ),
        check_vma=False,
    )
```

```python
import jax
import jax.numpy as jnp
from jax import lax
from jax.experimental import pallas as pl
from jax.experimental.pallas import tpu as pltpu
from jax.sharding import PartitionSpec as P

MESH = pl.DeviceIdType.MESH
F32, BF16 = jnp.float32, jnp.bfloat16

TOK, D, FS, CAP, NB, TOPK = 128, 3072, 672, 48, 16, 4
DS = D // 8
SLOTS = NB * CAP
CH = 256
NCH = SLOTS // CH

REL = [
    (0, 0), (0, 1), (1, 0), (0, 3), (3, 0), (0, 2), (2, 0),
    (1, 1), (3, 3), (1, 3), (3, 1), (1, 2), (2, 1), (3, 2), (2, 3), (2, 2),
]
OWN = 0
GROUPS = [(7, 11), (11, 16)]
NEAR = (0, 7)
FAR_LIST = [*range(*GROUPS[0]), *range(*GROUPS[1])]
NEAR_LIST = [q for q in range(*NEAR) if q != OWN]
OTHERS = [*range(*GROUPS[0]), *NEAR_LIST, *range(*GROUPS[1])]
N0, NR = NEAR[0] * CAP, (NEAR[1] - NEAR[0]) * CAP
NEAR_ROWS = [(0, 256), (256, NR)]
NEAR_RETURNS = [(0, 5), (5, 7)]
RING_ROWS = [None, ((336, 96), (432, 80)), ((512, 128), (640, 128))]
FAR_RETURNS = [None, (7, 10), (10, 16)]


def split2(v):
    hi = v.astype(BF16)
    lo = (v - hi.astype(F32)).astype(BF16)
    return hi, lo


def nn(a, b):
    return lax.dot_general(a, b, (((1,), (0,)), ((), ())), preferred_element_type=F32)


def nt(a, b):
    return lax.dot_general(a, b, (((1,), (1,)), ((), ())), preferred_element_type=F32)


def tn(a, b):
    return lax.dot_general(a, b, (((0,), (0,)), ((), ())), preferred_element_type=F32)


class Sems:
    def __init__(self, send, recv):
        self.send, self.recv, self.names = send, recv, {}

    def index(self, name):
        return self.names.setdefault(name, len(self.names))


N_SEMS = 208


def main_kernel(
    tok_ref, dy_ref, routes_ref, gates_ref, wg_hbm, wu_hbm, wd_hbm,
    gtok_ref, ggate_ref, x_out, dg_out, du_out, down_out,
    xdy, raw, sel, selb, pick, cols, wg, wu, wd, act, slope, hid, hg, dg, du, stage, gsend, grecv, grow,
    gpart, gall, gback, ghome, dxf, dxb, sibr, rs_send, rs_recv, near_back, near_home,
    tsum, rows_back, home, send_sems, recv_sems, local_sems, load_sems, store_sems, stage_sems,
):
    dp, ex = lax.axis_index("dp"), lax.axis_index("expert")
    y, c = dp // 2, dp % 2
    x, z = ex // 4, ex % 4

    def dev(yy, cc, xx, zz):
        return (lax.rem(yy + 8, 4) * 2 + cc, lax.rem(xx + 8, 4) * 4 + lax.rem(zz + 8, 4))

    up, down, sib = dev(y + 1, c, x, z), dev(y - 1, c, x, z), dev(y, 1 - c, x, z)

    def toward(q):
        return dev(y, c, x - REL[q][0], z - REL[q][1])

    def origin(q):
        return dev(y, c, x + REL[q][0], z + REL[q][1])

    def peer(i):
        return (lax.rem(dp + i, 8), ex)

    sems = Sems(send_sems, recv_sems)
    sent = []

    def copy(name, src, dst, device):
        i = sems.index(name)
        return pltpu.make_async_remote_copy(
            src, dst, sems.send.at[i], sems.recv.at[i], device_id=device, device_id_type=MESH
        )

    def send(name, src, dst, device):
        cp = copy(name, src, dst, device)
        cp.start()
        sent.append(cp)

    def drain(rest):
        while len(sent) > rest:
            sent.pop(0).wait_send()

    def arrive(name, dst, device):
        copy(name, dst, dst, device).wait_recv()

    barrier = pltpu.get_barrier_semaphore()
    partners = [toward(q) for q in OTHERS] + [peer(i) for i in range(1, 8)]
    for p in partners:
        pl.semaphore_signal(barrier, inc=1, device_id=p, device_id_type=MESH)

    def stored(k, cc):
        return pl.ds(pl.multiple_of((lax.rem(y + k, 4) * 2 + cc) * DS, 128), DS)

    loads = []

    def load_weights():
        for i, (src, dst) in enumerate(((wg_hbm, wg), (wu_hbm, wu), (wd_hbm, wd))):
            for k in range(4):
                for cc in range(2):
                    cp = pltpu.make_async_copy(
                        src.at[0, :, stored(k, cc)],
                        dst.at[:, pl.ds((cc * 4 + k) * DS, DS)],
                        load_sems.at[i * 8 + k * 2 + cc],
                    )
                    cp.start()
                    loads.append(cp)

    def feat(k):
        return pl.ds(pl.multiple_of((c * 4 + k) * DS, 128), DS)

    def feat_sib(k):
        return pl.ds(pl.multiple_of(((1 - c) * 4 + k) * DS, 128), DS)

    def block(q):
        return pl.ds(q * CAP, CAP)

    T1, T2 = pl.ds(0, TOK // 2), pl.ds(TOK // 2, TOK // 2)
    raw[0, 0] = tok_ref[...]
    raw[0, 1] = dy_ref[...]

    r_i = lax.broadcasted_iota(jnp.int32, (TOK, TOK), 0)
    c_i = lax.broadcasted_iota(jnp.int32, (TOK, TOK), 1)
    earlier = (r_i < c_i).astype(BF16)
    rt = routes_ref[...]
    gt = gates_ref[...].astype(F32)
    code = ((x + 4 - rt // 4) % 4) * 4 + (z + 4 - rt % 4) % 4
    marks = [(code == a * 4 + b) for a, b in REL]
    count = jnp.concatenate([jnp.sum(m.astype(F32), axis=0, keepdims=True) for m in marks], axis=0)
    gate_of = jnp.concatenate(
        [jnp.sum(jnp.where(m, gt, 0.0), axis=0, keepdims=True) for m in marks], axis=0
    )
    place = nn(count.astype(BF16), earlier)
    place = jnp.where(count > 0, place, -1.0).astype(BF16)
    s_col = lax.broadcasted_iota(jnp.int32, (SLOTS, NB), 0)
    q_col = lax.broadcasted_iota(jnp.int32, (SLOTS, NB), 1)
    spread = ((s_col >= q_col * CAP) & (s_col < q_col * CAP + CAP)).astype(BF16)
    s_row = lax.broadcasted_iota(jnp.int32, (NB, SLOTS), 1)
    q_row = lax.broadcasted_iota(jnp.int32, (NB, SLOTS), 0)
    spread_t = (s_row >= q_row * CAP) & (s_row < q_row * CAP + CAP)
    s_full = lax.broadcasted_iota(jnp.int32, (SLOTS, TOK), 0).astype(F32)
    within = s_full - CAP * jnp.floor((s_full + 0.5) * (1.0 / CAP))
    lane = lax.broadcasted_iota(jnp.int32, (SLOTS, TOK), 1).astype(F32)
    pick[...] = (nn(spread, place) == within).astype(BF16)

    def raw_send(a):
        send(("raw_up", a), raw.at[0, a], raw.at[3, a], up)
        send(("raw_down", a), raw.at[0, a], raw.at[1, a], down)

    def select(a):
        sel[a] = nn(pick[...], raw[0, a]).astype(BF16)

    own = {}

    def own_block(src, a, k):
        cp = pltpu.make_async_copy(src, xdy.at[a, block(OWN), feat(k)], local_sems.at[a * 4 + k])
        cp.start()
        own[a, k] = cp

    def rows_send(a, blocks):
        for q in blocks:
            if q == OWN:
                own_block(sel.at[a, block(OWN)], a, 0)
            else:
                send(("x", q, a), sel.at[a, block(q)], xdy.at[a, block(q), feat(0)], toward(q))

    def gates_send():
        cols[...] = (within == lane).astype(BF16)
        gate_slots = jnp.where(spread_t, nt(gate_of.astype(BF16), pick[...]), 0.0)
        gate_slots = nn(gate_slots.astype(BF16), cols[...])
        for q in range(NB):
            gsend[q] = jnp.broadcast_to(gate_slots[q : q + 1], (8, TOK))
        for q in OTHERS:
            send(("g", q), gsend.at[q], grecv.at[q], toward(q))
        grecv[OWN] = gsend[OWN]

    near = pl.ds(N0, NR)

    def near_send(a, k):
        selb[k - 1, a] = nn(pick[near], raw[k, a]).astype(BF16)
        for q in NEAR_LIST:
            src = selb.at[k - 1, a, pl.ds(q * CAP - N0, CAP)]
            send(("n", q, k, a), src, xdy.at[a, block(q), feat(k)], toward(q))
        own_block(selb.at[k - 1, a, pl.ds(OWN * CAP - N0, CAP)], a, k)

    def raw_relay(a):
        arrive(("raw_up", a), raw.at[3, a], down)
        send(("raw_up2", a), raw.at[3, a, T1], raw.at[2, a, T1], up)
        arrive(("raw_down", a), raw.at[1, a], up)
        send(("raw_down2", a), raw.at[1, a, T2], raw.at[2, a, T2], down)

    def raw_end(a):
        arrive(("raw_up2", a), raw.at[2, a, T1], down)
        arrive(("raw_down2", a), raw.at[2, a, T2], up)

    def near_share(a, k):
        own[a, k].wait()
        for q in NEAR_LIST:
            name = ("x", q, a) if k == 0 else ("n", q, k, a)
            arrive(name, xdy.at[a, block(q), feat(k)], origin(q))
        mine = xdy.at[a, near, feat(k)]
        send(("nsib", k, a), mine, mine, sib)

    def near_end(a):
        for k in range(4):
            arrive(("nsib", k, a), xdy.at[a, near, feat_sib(k)], sib)

    def halves(g):
        a, b = GROUPS[g][0] * CAP, GROUPS[g][1] * CAP
        mid = a + (b - a + 31) // 32 * 16
        return pl.ds(a, b - a), pl.ds(a, mid - a), pl.ds(mid, b - mid)

    def gather_own(g, a):
        for q in range(*GROUPS[g]):
            arrive(("x", q, a), xdy.at[a, block(q), feat(0)], origin(q))
        full, _, _ = halves(g)
        mine = xdy.at[a, full, feat(0)]
        send(("up", g, a), mine, xdy.at[a, full, feat(3)], up)
        send(("down", g, a), mine, xdy.at[a, full, feat(1)], down)
        send(("sib", g, a), mine, mine, sib)

    def gather_relay(g, a):
        full, first, second = halves(g)
        below = xdy.at[a, full, feat(3)]
        arrive(("up", g, a), below, down)
        send(("up2", g, a), xdy.at[a, first, feat(3)], xdy.at[a, first, feat(2)], up)
        above = xdy.at[a, full, feat(1)]
        arrive(("down", g, a), above, up)
        send(("down2", g, a), xdy.at[a, second, feat(1)], xdy.at[a, second, feat(2)], down)
        send(("sibb", g, a), below, below, sib)
        send(("siba", g, a), above, above, sib)

    def gather_end(g, a):
        full, first, second = halves(g)
        far1, far2 = xdy.at[a, first, feat(2)], xdy.at[a, second, feat(2)]
        arrive(("up2", g, a), far1, down)
        send(("sib1", g, a), far1, far1, sib)
        arrive(("down2", g, a), far2, up)
        send(("sib2", g, a), far2, far2, sib)
        arrive(("sib", g, a), xdy.at[a, full, feat_sib(0)], sib)
        arrive(("sibb", g, a), xdy.at[a, full, feat_sib(3)], sib)
        arrive(("siba", g, a), xdy.at[a, full, feat_sib(1)], sib)
        arrive(("sib1", g, a), xdy.at[a, first, feat_sib(2)], sib)
        arrive(("sib2", g, a), xdy.at[a, second, feat_sib(2)], sib)

    stores = []

    def store(src, dst):
        cp = pltpu.make_async_copy(src, dst, store_sems.at[len(stores)])
        cp.start()
        stores.append(cp)

    half = FS // 2

    def gate_up(j):
        rows = pl.ds(j * CH, CH)

        def step(i, carry):
            units = pl.ds(pl.multiple_of(i * half, 16), half)
            pre_gate = nt(wg[units], xdy[0, rows])
            pre_up = nt(wu[units], xdy[0, rows])
            squash = jax.nn.sigmoid(pre_gate)
            activated = pre_gate * squash
            hid[units, rows] = (activated * pre_up).astype(BF16)
            act[j, units] = activated
            slope[j, units] = pre_up * squash * (1.0 + pre_gate * (1.0 - squash))
            return carry

        lax.fori_loop(0, 2, step, 0)
        for k in range(4):
            for cc in range(2):
                src = xdy.at[0, rows, pl.ds((cc * 4 + k) * DS, DS)]
                store(src, x_out.at[rows, stored(k, cc)])

    def hidden_grad(j):
        rows = pl.ds(j * CH, CH)

        def step(i, total):
            units = pl.ds(pl.multiple_of(i * half, 16), half)
            projected = nt(wd[units], xdy[1, rows])
            hidden = hid[units, rows].astype(F32)
            gates = grow[0:1, rows]
            hg[units, rows] = (hidden * gates).astype(BF16)
            grad = gates * projected
            dg[units, rows] = (grad * slope[j, units]).astype(BF16)
            du[units, rows] = (grad * act[j, units]).astype(BF16)
            return total + jnp.sum(projected * hidden, axis=0, keepdims=True)

        gpart[0:1, rows] = lax.fori_loop(0, 2, step, jnp.zeros((1, CH), F32))

    def input_grad(j, ks=(2, 0)):
        rows = pl.ds(j * CH, CH)
        for k in ks:
            for core in (1 - c, c):
                feats = pl.ds(pl.multiple_of((core * 4 + k) * DS, 128), 2 * DS)
                part = tn(dg[:, rows], wg[:, feats]) + tn(du[:, rows], wu[:, feats])
                if core is c:
                    dxf[k, rows] = part[:, :DS]
                    dxf[k + 1, rows] = part[:, DS:]
                else:
                    dxb[k, rows] = part[:, :DS].astype(BF16)
                    dxb[k + 1, rows] = part[:, DS:].astype(BF16)
                    pair = pl.ds(k, 2)
                    send(("dx", j, k), dxb.at[pair, rows], sibr.at[pair, rows], sib)

    def dx_arrive(j, k):
        arrive(("dx", j, k), sibr.at[pl.ds(k, 2), pl.ds(j * CH, CH)], sib)

    def pair_sum(k, rows):
        return dxf[k, rows] + sibr[k, rows].astype(F32)

    pieces = []

    def down_piece(i):
        if i >= 2:
            for cp in pieces[2 * (i - 2) : 2 * (i - 1)]:
                cp.wait()
        cc, k = i // 2, i % 2 * 2
        stage[i % 2] = nn(hg[...], xdy[1, :, pl.ds((cc * 4 + k) * DS, 2 * DS)]).astype(BF16)
        for m in range(2):
            cp = pltpu.make_async_copy(
                stage.at[i % 2, :, pl.ds(m * DS, DS)],
                down_out.at[:, stored(k + m, cc)],
                stage_sems.at[i * 2 + m],
            )
            cp.start()
            pieces.append(cp)

    class RingSum:
        def __init__(self, i, part, first, second):
            self.i, self.part, self.first, self.second = i, part, pl.ds(*first), pl.ds(*second)

        def buffer(self, ref, slot, rows):
            return ref.at[self.i, slot, pl.ds(0, rows.size)]

        def hop(self, name, slot, value, rows, device):
            src = self.buffer(rs_send, slot, rows)
            src[...] = value.astype(BF16)
            send((name, self.i), src, self.buffer(rs_recv, slot, rows), device)

        def take(self, name, slot, rows, device):
            dst = self.buffer(rs_recv, slot, rows)
            arrive((name, self.i), dst, device)
            return dst[...].astype(F32)

        def far(self):
            self.hop("f_up", 0, self.part(2, self.first), self.first, up)
            self.hop("f_down", 1, self.part(2, self.second), self.second, down)
            self.hop("d_down", 3, self.part(3, self.first), self.first, down)

        def near(self):
            self.hop("d_up", 2, self.part(1, self.second), self.second, up)

        def relay(self):
            got = self.take("f_up", 0, self.first, down)
            self.hop("e_up", 4, self.part(1, self.first) + got, self.first, up)
            got = self.take("f_down", 1, self.second, up)
            self.hop("e_down", 5, self.part(3, self.second) + got, self.second, down)

        def sums(self):
            a = self.part(0, self.first) + self.take("d_down", 3, self.first, up)
            a = a + self.take("e_up", 4, self.first, down)
            b = self.part(0, self.second) + self.take("d_up", 2, self.second, down)
            b = b + self.take("e_down", 5, self.second, up)
            return a, b

    rings = [r and RingSum(j, pair_sum, *r) for j, r in enumerate(RING_ROWS)]

    def scatter1(j):
        dx_arrive(j, 2)
        rings[j].far()
        dx_arrive(j, 0)
        rings[j].near()

    def scatter3(j):
        for value, rows in zip(rings[j].sums(), RING_ROWS[j]):
            rows_back[pl.ds(*rows)] = value.astype(BF16)
        for q in range(*FAR_RETURNS[j]):
            send(("r", q), rows_back.at[block(q)], home.at[block(q)], origin(q))

    def near_return(j):
        a, b = NEAR_ROWS[j]
        for k in range(4):
            near_back[k, pl.ds(a - N0, b - a)] = pair_sum(k, pl.ds(a, b - a)).astype(BF16)
        for q in range(*NEAR_RETURNS[j]):
            rows = pl.ds(q * CAP - N0, CAP)
            if q == OWN:
                near_home[:, rows] = near_back[:, rows]
            else:
                send(("nr", q), near_back.at[:, rows], near_home.at[:, rows], origin(q))

    def near_combine():
        for q in NEAR_LIST:
            arrive(("nr", q), near_home.at[:, pl.ds(q * CAP - N0, CAP)], toward(q))
        for k in (2, 1, 3, 0):
            tsum[k] = tn(pick[near], near_home[k])

    token_ring = RingSum(0, lambda k, rows: tsum[k, rows], (0, TOK // 2), (TOK // 2, TOK // 2))

    def gate_rows():
        for q in OTHERS:
            arrive(("g", q), grecv.at[q], origin(q))
        table = jnp.concatenate([grecv[q, 0:1] for q in range(NB)], axis=0)
        wide = jnp.where(spread_t, nt(table.astype(BF16), cols[...]), 0.0)
        grow[...] = jnp.broadcast_to(jnp.sum(wide, axis=0, keepdims=True), (8, SLOTS))

    def gate_sums():
        wide = jnp.where(spread_t, jnp.broadcast_to(gpart[0:1], (NB, SLOTS)), 0.0)
        h, l = split2(wide)
        gall[dp] = nn(h, cols[...]) + nn(l, cols[...])
        for i in range(1, 8):
            send(("ga", i), gall.at[dp], gall.at[dp], peer(i))

    def gate_back():
        for i in range(1, 8):
            arrive(("ga", i), gall.at[lax.rem(dp + 8 - i, 8)], peer(8 - i))
        total = gall[0]
        for i in range(1, 8):
            total = total + gall[i]
        for q in range(NB):
            gback[q] = jnp.broadcast_to(total[q : q + 1], (8, TOK))
        for q in OTHERS:
            send(("gr", q), gback.at[q], ghome.at[q], origin(q))
        ghome[OWN] = gback[OWN]

    def gate_end():
        for q in OTHERS:
            arrive(("gr", q), ghome.at[q], toward(q))
        table = jnp.concatenate([ghome[q, 0:1] for q in range(NB)], axis=0)
        h, l = split2(table)
        wide = jnp.where(spread_t, nt(h, cols[...]) + nt(l, cols[...]), 0.0)
        h, l = split2(wide)
        per_token = nn(h, pick[...]) + nn(l, pick[...])
        out = jnp.zeros((TOPK, TOK), F32)
        for q in range(NB):
            out = out + jnp.where(marks[q], jnp.broadcast_to(per_token[q : q + 1], (TOPK, TOK)), 0.0)
        ggate_ref[...] = out

    far0, far1, close = range(*GROUPS[0]), range(*GROUPS[1]), range(*NEAR)
    select(0)
    pl.semaphore_wait(barrier, len(partners))
    raw_send(0)
    rows_send(0, far0)
    rows_send(0, close)
    raw_send(1)
    rows_send(0, far1)
    select(1)
    load_weights()
    raw_relay(0)
    near_send(0, 3)
    near_send(0, 1)
    gather_own(0, 0)
    raw_relay(1)
    raw_end(0)
    near_send(0, 2)
    rows_send(1, far0)
    rows_send(1, close)
    gather_own(1, 0)
    near_send(1, 3)
    near_send(1, 1)
    gates_send()
    near_share(0, 0)
    rows_send(1, far1)
    raw_end(1)
    near_send(1, 2)
    gather_relay(0, 0)
    near_share(0, 3)
    near_share(0, 1)
    near_share(0, 2)
    near_end(0)
    for cp in loads:
        cp.wait()
    gather_own(0, 1)
    gate_up(0)
    gather_relay(1, 0)
    near_share(1, 0)
    gather_end(0, 0)
    gate_up(1)
    gather_relay(0, 1)
    gather_end(1, 0)
    near_share(1, 3)
    near_share(1, 1)
    gate_up(2)
    gate_rows()
    gather_own(1, 1)
    near_share(1, 2)
    drain(60)
    near_end(1)
    hidden_grad(0)
    input_grad(0)
    gather_relay(1, 1)
    gather_end(0, 1)
    hidden_grad(1)
    dx_arrive(0, 2)
    dx_arrive(0, 0)
    near_return(0)
    input_grad(1)
    gather_end(1, 1)
    hidden_grad(2)
    gate_sums()
    dx_arrive(1, 2)
    rings[1].far()
    dx_arrive(1, 0)
    rings[1].near()
    near_return(1)
    input_grad(2, (2,))
    rings[1].relay()
    input_grad(2, (0,))
    dx_arrive(2, 2)
    rings[2].far()
    dx_arrive(2, 0)
    rings[2].near()
    gate_back()
    store(dg, dg_out)
    store(du, du_out)
    scatter3(1)
    rings[2].relay()
    near_combine()
    token_ring.far()
    token_ring.near()
    down_piece(0)
    gate_end()
    drain(50)
    scatter3(2)
    token_ring.relay()
    down_piece(1)
    down_piece(2)
    down_piece(3)
    first, second = token_ring.sums()
    for q in FAR_LIST:
        arrive(("r", q), home.at[block(q)], toward(q))
    far_sum = jnp.zeros((TOK, DS), F32)
    for a, b in GROUPS:
        rows = pl.ds(a * CAP, (b - a) * CAP)
        far_sum = far_sum + tn(pick[rows], home[rows])
    gtok_ref[T1] = (far_sum[: TOK // 2] + first).astype(BF16)
    gtok_ref[T2] = (far_sum[TOK // 2 :] + second).astype(BF16)
    for cp in pieces[4:]:
        cp.wait()
    for cp in sent:
        cp.wait_send()
    for cp in stores:
        cp.wait()


def exchange(tokens, grad_out, routes, gates, w_gate, w_up, w_down):
    vmem = pl.BlockSpec(memory_space=pltpu.VMEM)
    hbm = pl.BlockSpec(memory_space=pl.ANY)
    return pl.pallas_call(
        main_kernel,
        out_shape=(
            jax.ShapeDtypeStruct((TOK, DS), BF16),
            jax.ShapeDtypeStruct((TOPK, TOK), F32),
            jax.ShapeDtypeStruct((SLOTS, D), BF16),
            jax.ShapeDtypeStruct((FS, SLOTS), BF16),
            jax.ShapeDtypeStruct((FS, SLOTS), BF16),
            jax.ShapeDtypeStruct((FS, D), BF16),
        ),
        in_specs=[vmem] * 4 + [hbm] * 3,
        out_specs=(vmem, vmem, hbm, hbm, hbm, hbm),
        scratch_shapes=[
            pltpu.VMEM((2, SLOTS, D), BF16),
            pltpu.VMEM((4, 2, TOK, DS), BF16),
            pltpu.VMEM((2, SLOTS, DS), BF16),
            pltpu.VMEM((3, 2, NR, DS), BF16),
            pltpu.VMEM((SLOTS, TOK), BF16),
            pltpu.VMEM((SLOTS, TOK), BF16),
            pltpu.VMEM((FS, D), BF16),
            pltpu.VMEM((FS, D), BF16),
            pltpu.VMEM((FS, D), BF16),
            pltpu.VMEM((NCH, FS, CH), F32),
            pltpu.VMEM((NCH, FS, CH), F32),
            pltpu.VMEM((FS, SLOTS), BF16),
            pltpu.VMEM((FS, SLOTS), BF16),
            pltpu.VMEM((FS, SLOTS), BF16),
            pltpu.VMEM((FS, SLOTS), BF16),
            pltpu.VMEM((2, FS, 2 * DS), BF16),
            pltpu.VMEM((NB, 8, TOK), F32),
            pltpu.VMEM((NB, 8, TOK), F32),
            pltpu.VMEM((8, SLOTS), F32),
            pltpu.VMEM((8, SLOTS), F32),
            pltpu.VMEM((8, NB, TOK), F32),
            pltpu.VMEM((NB, 8, TOK), F32),
            pltpu.VMEM((NB, 8, TOK), F32),
            pltpu.VMEM((4, SLOTS, DS), F32),
            pltpu.VMEM((4, SLOTS, DS), BF16),
            pltpu.VMEM((4, SLOTS, DS), BF16),
            pltpu.VMEM((3, 6, CH // 2, DS), BF16),
            pltpu.VMEM((3, 6, CH // 2, DS), BF16),
            pltpu.VMEM((4, NR, DS), BF16),
            pltpu.VMEM((4, NR, DS), BF16),
            pltpu.VMEM((4, TOK, DS), F32),
            pltpu.VMEM((SLOTS, DS), BF16),
            pltpu.VMEM((SLOTS, DS), BF16),
            pltpu.SemaphoreType.DMA((N_SEMS,)),
            pltpu.SemaphoreType.DMA((N_SEMS,)),
            pltpu.SemaphoreType.DMA((8,)),
            pltpu.SemaphoreType.DMA((24,)),
            pltpu.SemaphoreType.DMA((26,)),
            pltpu.SemaphoreType.DMA((8,)),
        ],
        compiler_params=pltpu.CompilerParams(
            collective_id=0, has_side_effects=True, vmem_limit_bytes=60 << 20
        ),
        cost_estimate=pl.CostEstimate(
            flops=2 * 5 * SLOTS * FS * D, bytes_accessed=25_000_000, transcendentals=SLOTS * FS
        ),
    )(tokens, grad_out, routes.T, gates.T, w_gate, w_up, w_down)


def weight_kernel(
    tok_ref, gate_ref, x_ref, dg_ref, du_ref, down_ref, tok_out, gate_out, og_ref, ou_ref, od_ref
):
    @pl.when(pl.program_id(0) == 0)
    def _():
        tok_out[...] = tok_ref[...]
        gate_out[...] = gate_ref[...]

    og_ref[0] = nn(dg_ref[...], x_ref[...]).astype(BF16)
    ou_ref[0] = nn(du_ref[...], x_ref[...]).astype(BF16)
    od_ref[0] = down_ref[...]


def weight_grads(grad_tokens, grad_gates, x, dg, du, down):
    tile = 768
    whole = pl.BlockSpec((FS, SLOTS), lambda i: (0, 0))
    small = [pl.BlockSpec(a.shape, lambda i: (0, 0)) for a in (grad_tokens, grad_gates)]
    out = pl.BlockSpec((1, FS, tile), lambda i: (0, 0, i))
    shape = jax.ShapeDtypeStruct((1, FS, D), BF16)
    return pl.pallas_call(
        weight_kernel,
        grid=(D // tile,),
        out_shape=(
            jax.ShapeDtypeStruct(grad_tokens.shape, BF16),
            jax.ShapeDtypeStruct(grad_gates.shape, F32),
            shape, shape, shape,
        ),
        in_specs=[
            *small,
            pl.BlockSpec((SLOTS, tile), lambda i: (0, i)),
            whole,
            whole,
            pl.BlockSpec((FS, tile), lambda i: (0, i)),
        ],
        out_specs=(*small, out, out, out),
        compiler_params=pltpu.CompilerParams(vmem_limit_bytes=62 << 20),
        cost_estimate=pl.CostEstimate(
            flops=2 * 2 * SLOTS * FS * D, bytes_accessed=25_000_000, transcendentals=0
        ),
    )(grad_tokens, grad_gates, x, dg, du, down)


def per_device(tokens, grad_out, routes, gate_values, w_gate, w_up, w_down):
    grad_tokens, grad_gates, x, dg, du, down = exchange(
        tokens, grad_out, routes, gate_values, w_gate, w_up, w_down
    )
    grad_tokens, grad_gates, grad_w_gate, grad_w_up, grad_w_down = weight_grads(
        grad_tokens, grad_gates, x, dg, du, down
    )
    return grad_tokens, grad_gates.T, grad_w_gate, grad_w_up, grad_w_down


def solution(mesh):
    return jax.shard_map(
        per_device,
        mesh=mesh,
        in_specs=(
            P("expert", "dp"),
            P("expert", "dp"),
            P("expert", None),
            P("expert", None),
            P("expert", "dp", None),
            P("expert", "dp", None),
            P("expert", "dp", None),
        ),
        out_specs=(
            P("expert", "dp"),
            P("expert", None),
            P("expert", "dp", None),
            P("expert", "dp", None),
            P("expert", "dp", None),
        ),
        check_vma=False,
    )
```

```python
import jax
import jax.numpy as jnp
from jax import lax
from jax.experimental import pallas as pl
from jax.experimental.pallas import tpu as pltpu
from jax.sharding import PartitionSpec as P

MESH = pl.DeviceIdType.MESH
F32, BF16 = jnp.float32, jnp.bfloat16

TOK, D, FS, CAP, NB, TOPK = 128, 3072, 672, 48, 16, 4
DS = D // 8
SLOTS = NB * CAP
CH = 256
NCH = SLOTS // CH

REL = [
    (0, 0), (0, 1), (1, 0), (0, 3), (3, 0), (0, 2), (2, 0),
    (1, 1), (3, 3), (1, 3), (3, 1), (1, 2), (2, 1), (3, 2), (2, 3), (2, 2),
]
OWN = 0
GROUPS = [(7, 11), (11, 16)]
NEAR = (0, 7)
FAR_LIST = [*range(*GROUPS[0]), *range(*GROUPS[1])]
NEAR_LIST = [q for q in range(*NEAR) if q != OWN]
OTHERS = [*range(*GROUPS[0]), *NEAR_LIST, *range(*GROUPS[1])]
N0, NR = NEAR[0] * CAP, (NEAR[1] - NEAR[0]) * CAP
NEAR_ROWS = [(0, 256), (256, NR)]
NEAR_RETURNS = [(0, 5), (5, 7)]
RING_ROWS = [None, ((336, 96), (432, 80)), ((512, 128), (640, 128))]
FAR_RETURNS = [None, (7, 10), (10, 16)]


def split2(v):
    hi = v.astype(BF16)
    lo = (v - hi.astype(F32)).astype(BF16)
    return hi, lo


def nn(a, b):
    return lax.dot_general(a, b, (((1,), (0,)), ((), ())), preferred_element_type=F32)


def nt(a, b):
    return lax.dot_general(a, b, (((1,), (1,)), ((), ())), preferred_element_type=F32)


def tn(a, b):
    return lax.dot_general(a, b, (((0,), (0,)), ((), ())), preferred_element_type=F32)


class Sems:
    def __init__(self, send, recv):
        self.send, self.recv, self.names = send, recv, {}

    def index(self, name):
        return self.names.setdefault(name, len(self.names))


N_SEMS = 208


def main_kernel(
    tok_ref, dy_ref, routes_ref, gates_ref, wg_hbm, wu_hbm, wd_hbm,
    gtok_ref, ggate_ref, x_out, dg_out, du_out, down_out,
    xdy, raw, sel, selb, pick, cols, wg, wu, wd, act, slope, hid, hg, dg, du, stage, gsend, grecv, grow,
    gpart, gall, gback, ghome, dxf, dxb, sibr, rs_send, rs_recv, near_back, near_home,
    tsum, rows_back, home, send_sems, recv_sems, local_sems, load_sems, store_sems, stage_sems,
):
    dp, ex = lax.axis_index("dp"), lax.axis_index("expert")
    y, c = dp // 2, dp % 2
    x, z = ex // 4, ex % 4

    def dev(yy, cc, xx, zz):
        return (lax.rem(yy + 8, 4) * 2 + cc, lax.rem(xx + 8, 4) * 4 + lax.rem(zz + 8, 4))

    up, down, sib = dev(y + 1, c, x, z), dev(y - 1, c, x, z), dev(y, 1 - c, x, z)

    def toward(q):
        return dev(y, c, x - REL[q][0], z - REL[q][1])

    def origin(q):
        return dev(y, c, x + REL[q][0], z + REL[q][1])

    def peer(i):
        return (lax.rem(dp + i, 8), ex)

    sems = Sems(send_sems, recv_sems)
    sent = []

    def copy(name, src, dst, device):
        i = sems.index(name)
        return pltpu.make_async_remote_copy(
            src, dst, sems.send.at[i], sems.recv.at[i], device_id=device, device_id_type=MESH
        )

    def send(name, src, dst, device):
        cp = copy(name, src, dst, device)
        cp.start()
        sent.append(cp)

    def drain(rest):
        while len(sent) > rest:
            sent.pop(0).wait_send()

    def arrive(name, dst, device):
        copy(name, dst, dst, device).wait_recv()

    barrier = pltpu.get_barrier_semaphore()
    partners = [toward(q) for q in OTHERS] + [peer(i) for i in range(1, 8)]
    for p in partners:
        pl.semaphore_signal(barrier, inc=1, device_id=p, device_id_type=MESH)

    def stored(k, cc):
        return pl.ds(pl.multiple_of((lax.rem(y + k, 4) * 2 + cc) * DS, 128), DS)

    loads = []

    def load_weights():
        for i, (src, dst) in enumerate(((wg_hbm, wg), (wu_hbm, wu), (wd_hbm, wd))):
            for k in range(4):
                for cc in range(2):
                    cp = pltpu.make_async_copy(
                        src.at[0, :, stored(k, cc)],
                        dst.at[:, pl.ds((cc * 4 + k) * DS, DS)],
                        load_sems.at[i * 8 + k * 2 + cc],
                    )
                    cp.start()
                    loads.append(cp)

    def feat(k):
        return pl.ds(pl.multiple_of((c * 4 + k) * DS, 128), DS)

    def feat_sib(k):
        return pl.ds(pl.multiple_of(((1 - c) * 4 + k) * DS, 128), DS)

    def block(q):
        return pl.ds(q * CAP, CAP)

    T1, T2 = pl.ds(0, TOK // 2), pl.ds(TOK // 2, TOK // 2)
    raw[0, 0] = tok_ref[...]
    raw[0, 1] = dy_ref[...]

    r_i = lax.broadcasted_iota(jnp.int32, (TOK, TOK), 0)
    c_i = lax.broadcasted_iota(jnp.int32, (TOK, TOK), 1)
    earlier = (r_i < c_i).astype(BF16)
    rt = routes_ref[...]
    gt = gates_ref[...].astype(F32)
    code = ((x + 4 - rt // 4) % 4) * 4 + (z + 4 - rt % 4) % 4
    marks = [(code == a * 4 + b) for a, b in REL]
    count = jnp.concatenate([jnp.sum(m.astype(F32), axis=0, keepdims=True) for m in marks], axis=0)
    gate_of = jnp.concatenate(
        [jnp.sum(jnp.where(m, gt, 0.0), axis=0, keepdims=True) for m in marks], axis=0
    )
    place = nn(count.astype(BF16), earlier)
    place = jnp.where(count > 0, place, -1.0).astype(BF16)
    s_col = lax.broadcasted_iota(jnp.int32, (SLOTS, NB), 0)
    q_col = lax.broadcasted_iota(jnp.int32, (SLOTS, NB), 1)
    spread = ((s_col >= q_col * CAP) & (s_col < q_col * CAP + CAP)).astype(BF16)
    s_row = lax.broadcasted_iota(jnp.int32, (NB, SLOTS), 1)
    q_row = lax.broadcasted_iota(jnp.int32, (NB, SLOTS), 0)
    spread_t = (s_row >= q_row * CAP) & (s_row < q_row * CAP + CAP)
    s_full = lax.broadcasted_iota(jnp.int32, (SLOTS, TOK), 0).astype(F32)
    within = s_full - CAP * jnp.floor((s_full + 0.5) * (1.0 / CAP))
    lane = lax.broadcasted_iota(jnp.int32, (SLOTS, TOK), 1).astype(F32)
    pick[...] = (nn(spread, place) == within).astype(BF16)

    def raw_send(a):
        send(("raw_up", a), raw.at[0, a], raw.at[3, a], up)
        send(("raw_down", a), raw.at[0, a], raw.at[1, a], down)

    def select(a):
        sel[a] = nn(pick[...], raw[0, a]).astype(BF16)

    own = {}

    def own_block(src, a, k):
        cp = pltpu.make_async_copy(src, xdy.at[a, block(OWN), feat(k)], local_sems.at[a * 4 + k])
        cp.start()
        own[a, k] = cp

    def rows_send(a, blocks):
        for q in blocks:
            if q == OWN:
                own_block(sel.at[a, block(OWN)], a, 0)
            else:
                send(("x", q, a), sel.at[a, block(q)], xdy.at[a, block(q), feat(0)], toward(q))

    def gates_send():
        cols[...] = (within == lane).astype(BF16)
        gate_slots = jnp.where(spread_t, nt(gate_of.astype(BF16), pick[...]), 0.0)
        gate_slots = nn(gate_slots.astype(BF16), cols[...])
        for q in range(NB):
            gsend[q] = jnp.broadcast_to(gate_slots[q : q + 1], (8, TOK))
        for q in OTHERS:
            send(("g", q), gsend.at[q], grecv.at[q], toward(q))
        grecv[OWN] = gsend[OWN]

    near = pl.ds(N0, NR)

    def near_send(a, k):
        selb[k - 1, a] = nn(pick[near], raw[k, a]).astype(BF16)
        for q in NEAR_LIST:
            src = selb.at[k - 1, a, pl.ds(q * CAP - N0, CAP)]
            send(("n", q, k, a), src, xdy.at[a, block(q), feat(k)], toward(q))
        own_block(selb.at[k - 1, a, pl.ds(OWN * CAP - N0, CAP)], a, k)

    def raw_relay(a):
        arrive(("raw_up", a), raw.at[3, a], down)
        send(("raw_up2", a), raw.at[3, a, T1], raw.at[2, a, T1], up)
        arrive(("raw_down", a), raw.at[1, a], up)
        send(("raw_down2", a), raw.at[1, a, T2], raw.at[2, a, T2], down)

    def raw_end(a):
        arrive(("raw_up2", a), raw.at[2, a, T1], down)
        arrive(("raw_down2", a), raw.at[2, a, T2], up)

    def near_share(a, k):
        own[a, k].wait()
        for q in NEAR_LIST:
            name = ("x", q, a) if k == 0 else ("n", q, k, a)
            arrive(name, xdy.at[a, block(q), feat(k)], origin(q))
        mine = xdy.at[a, near, feat(k)]
        send(("nsib", k, a), mine, mine, sib)

    def near_end(a):
        for k in range(4):
            arrive(("nsib", k, a), xdy.at[a, near, feat_sib(k)], sib)

    def halves(g):
        a, b = GROUPS[g][0] * CAP, GROUPS[g][1] * CAP
        mid = a + (b - a + 31) // 32 * 16
        return pl.ds(a, b - a), pl.ds(a, mid - a), pl.ds(mid, b - mid)

    def gather_own(g, a):
        for q in range(*GROUPS[g]):
            arrive(("x", q, a), xdy.at[a, block(q), feat(0)], origin(q))
        full, _, _ = halves(g)
        mine = xdy.at[a, full, feat(0)]
        send(("up", g, a), mine, xdy.at[a, full, feat(3)], up)
        send(("down", g, a), mine, xdy.at[a, full, feat(1)], down)
        send(("sib", g, a), mine, mine, sib)

    def gather_relay(g, a):
        full, first, second = halves(g)
        below = xdy.at[a, full, feat(3)]
        arrive(("up", g, a), below, down)
        send(("up2", g, a), xdy.at[a, first, feat(3)], xdy.at[a, first, feat(2)], up)
        above = xdy.at[a, full, feat(1)]
        arrive(("down", g, a), above, up)
        send(("down2", g, a), xdy.at[a, second, feat(1)], xdy.at[a, second, feat(2)], down)
        send(("sibb", g, a), below, below, sib)
        send(("siba", g, a), above, above, sib)

    def gather_end(g, a):
        full, first, second = halves(g)
        far1, far2 = xdy.at[a, first, feat(2)], xdy.at[a, second, feat(2)]
        arrive(("up2", g, a), far1, down)
        send(("sib1", g, a), far1, far1, sib)
        arrive(("down2", g, a), far2, up)
        send(("sib2", g, a), far2, far2, sib)
        arrive(("sib", g, a), xdy.at[a, full, feat_sib(0)], sib)
        arrive(("sibb", g, a), xdy.at[a, full, feat_sib(3)], sib)
        arrive(("siba", g, a), xdy.at[a, full, feat_sib(1)], sib)
        arrive(("sib1", g, a), xdy.at[a, first, feat_sib(2)], sib)
        arrive(("sib2", g, a), xdy.at[a, second, feat_sib(2)], sib)

    stores = []

    def store(src, dst):
        cp = pltpu.make_async_copy(src, dst, store_sems.at[len(stores)])
        cp.start()
        stores.append(cp)

    half = FS // 2

    def gate_up(j):
        rows = pl.ds(j * CH, CH)

        def step(i, carry):
            units = pl.ds(pl.multiple_of(i * half, 16), half)
            pre_gate = nt(wg[units], xdy[0, rows])
            pre_up = nt(wu[units], xdy[0, rows])
            squash = jax.nn.sigmoid(pre_gate)
            activated = pre_gate * squash
            hid[units, rows] = (activated * pre_up).astype(BF16)
            act[j, units] = activated
            slope[j, units] = pre_up * squash * (1.0 + pre_gate * (1.0 - squash))
            return carry

        lax.fori_loop(0, 2, step, 0)
        for k in range(4):
            for cc in range(2):
                src = xdy.at[0, rows, pl.ds((cc * 4 + k) * DS, DS)]
                store(src, x_out.at[rows, stored(k, cc)])

    def hidden_grad(j):
        rows = pl.ds(j * CH, CH)

        def step(i, total):
            units = pl.ds(pl.multiple_of(i * half, 16), half)
            projected = nt(wd[units], xdy[1, rows])
            hidden = hid[units, rows].astype(F32)
            gates = grow[0:1, rows]
            hg[units, rows] = (hidden * gates).astype(BF16)
            grad = gates * projected
            dg[units, rows] = (grad * slope[j, units]).astype(BF16)
            du[units, rows] = (grad * act[j, units]).astype(BF16)
            return total + jnp.sum(projected * hidden, axis=0, keepdims=True)

        gpart[0:1, rows] = lax.fori_loop(0, 2, step, jnp.zeros((1, CH), F32))

    def input_grad(j, ks=(2, 0)):
        rows = pl.ds(j * CH, CH)
        for k in ks:
            for core in (1 - c, c):
                feats = pl.ds(pl.multiple_of((core * 4 + k) * DS, 128), 2 * DS)
                part = tn(dg[:, rows], wg[:, feats]) + tn(du[:, rows], wu[:, feats])
                if core is c:
                    dxf[k, rows] = part[:, :DS]
                    dxf[k + 1, rows] = part[:, DS:]
                else:
                    dxb[k, rows] = part[:, :DS].astype(BF16)
                    dxb[k + 1, rows] = part[:, DS:].astype(BF16)
                    pair = pl.ds(k, 2)
                    send(("dx", j, k), dxb.at[pair, rows], sibr.at[pair, rows], sib)

    def dx_arrive(j, k):
        arrive(("dx", j, k), sibr.at[pl.ds(k, 2), pl.ds(j * CH, CH)], sib)

    def pair_sum(k, rows):
        return dxf[k, rows] + sibr[k, rows].astype(F32)

    pieces = []

    def down_piece(i):
        if i >= 2:
            for cp in pieces[2 * (i - 2) : 2 * (i - 1)]:
                cp.wait()
        cc, k = i // 2, i % 2 * 2
        stage[i % 2] = nn(hg[...], xdy[1, :, pl.ds((cc * 4 + k) * DS, 2 * DS)]).astype(BF16)
        for m in range(2):
            cp = pltpu.make_async_copy(
                stage.at[i % 2, :, pl.ds(m * DS, DS)],
                down_out.at[:, stored(k + m, cc)],
                stage_sems.at[i * 2 + m],
            )
            cp.start()
            pieces.append(cp)

    class RingSum:
        def __init__(self, i, part, first, second):
            self.i, self.part, self.first, self.second = i, part, pl.ds(*first), pl.ds(*second)

        def buffer(self, ref, slot, rows):
            return ref.at[self.i, slot, pl.ds(0, rows.size)]

        def hop(self, name, slot, value, rows, device):
            src = self.buffer(rs_send, slot, rows)
            src[...] = value.astype(BF16)
            send((name, self.i), src, self.buffer(rs_recv, slot, rows), device)

        def take(self, name, slot, rows, device):
            dst = self.buffer(rs_recv, slot, rows)
            arrive((name, self.i), dst, device)
            return dst[...].astype(F32)

        def far(self):
            self.hop("f_up", 0, self.part(2, self.first), self.first, up)
            self.hop("f_down", 1, self.part(2, self.second), self.second, down)
            self.hop("d_down", 3, self.part(3, self.first), self.first, down)

        def near(self):
            self.hop("d_up", 2, self.part(1, self.second), self.second, up)

        def relay(self):
            got = self.take("f_up", 0, self.first, down)
            self.hop("e_up", 4, self.part(1, self.first) + got, self.first, up)
            got = self.take("f_down", 1, self.second, up)
            self.hop("e_down", 5, self.part(3, self.second) + got, self.second, down)

        def sums(self):
            a = self.part(0, self.first) + self.take("d_down", 3, self.first, up)
            a = a + self.take("e_up", 4, self.first, down)
            b = self.part(0, self.second) + self.take("d_up", 2, self.second, down)
            b = b + self.take("e_down", 5, self.second, up)
            return a, b

    rings = [r and RingSum(j, pair_sum, *r) for j, r in enumerate(RING_ROWS)]

    def scatter1(j):
        dx_arrive(j, 2)
        rings[j].far()
        dx_arrive(j, 0)
        rings[j].near()

    def scatter3(j):
        for value, rows in zip(rings[j].sums(), RING_ROWS[j]):
            rows_back[pl.ds(*rows)] = value.astype(BF16)
        for q in range(*FAR_RETURNS[j]):
            send(("r", q), rows_back.at[block(q)], home.at[block(q)], origin(q))

    def near_return(j):
        a, b = NEAR_ROWS[j]
        for k in range(4):
            near_back[k, pl.ds(a - N0, b - a)] = pair_sum(k, pl.ds(a, b - a)).astype(BF16)
        for q in range(*NEAR_RETURNS[j]):
            rows = pl.ds(q * CAP - N0, CAP)
            if q == OWN:
                near_home[:, rows] = near_back[:, rows]
            else:
                send(("nr", q), near_back.at[:, rows], near_home.at[:, rows], origin(q))

    def near_combine():
        for q in NEAR_LIST:
            arrive(("nr", q), near_home.at[:, pl.ds(q * CAP - N0, CAP)], toward(q))
        for k in (2, 1, 3, 0):
            tsum[k] = tn(pick[near], near_home[k])

    token_ring = RingSum(0, lambda k, rows: tsum[k, rows], (0, TOK // 2), (TOK // 2, TOK // 2))

    def gate_rows():
        for q in OTHERS:
            arrive(("g", q), grecv.at[q], origin(q))
        table = jnp.concatenate([grecv[q, 0:1] for q in range(NB)], axis=0)
        wide = jnp.where(spread_t, nt(table.astype(BF16), cols[...]), 0.0)
        grow[...] = jnp.broadcast_to(jnp.sum(wide, axis=0, keepdims=True), (8, SLOTS))

    def gate_sums():
        wide = jnp.where(spread_t, jnp.broadcast_to(gpart[0:1], (NB, SLOTS)), 0.0)
        h, l = split2(wide)
        gall[dp] = nn(h, cols[...]) + nn(l, cols[...])
        for i in range(1, 8):
            send(("ga", i), gall.at[dp], gall.at[dp], peer(i))

    def gate_back():
        for i in range(1, 8):
            arrive(("ga", i), gall.at[lax.rem(dp + 8 - i, 8)], peer(8 - i))
        total = gall[0]
        for i in range(1, 8):
            total = total + gall[i]
        for q in range(NB):
            gback[q] = jnp.broadcast_to(total[q : q + 1], (8, TOK))
        for q in OTHERS:
            send(("gr", q), gback.at[q], ghome.at[q], origin(q))
        ghome[OWN] = gback[OWN]

    def gate_end():
        for q in OTHERS:
            arrive(("gr", q), ghome.at[q], toward(q))
        table = jnp.concatenate([ghome[q, 0:1] for q in range(NB)], axis=0)
        h, l = split2(table)
        wide = jnp.where(spread_t, nt(h, cols[...]) + nt(l, cols[...]), 0.0)
        h, l = split2(wide)
        per_token = nn(h, pick[...]) + nn(l, pick[...])
        out = jnp.zeros((TOPK, TOK), F32)
        for q in range(NB):
            out = out + jnp.where(marks[q], jnp.broadcast_to(per_token[q : q + 1], (TOPK, TOK)), 0.0)
        ggate_ref[...] = out

    far0, far1, close = range(*GROUPS[0]), range(*GROUPS[1]), range(*NEAR)
    select(0)
    pl.semaphore_wait(barrier, len(partners))
    raw_send(0)
    rows_send(0, far0)
    rows_send(0, close)
    raw_send(1)
    rows_send(0, far1)
    select(1)
    load_weights()
    raw_relay(0)
    near_send(0, 3)
    near_send(0, 1)
    gather_own(0, 0)
    raw_relay(1)
    raw_end(0)
    near_send(0, 2)
    rows_send(1, far0)
    rows_send(1, close)
    gather_own(1, 0)
    near_send(1, 3)
    near_send(1, 1)
    gates_send()
    near_share(0, 0)
    rows_send(1, far1)
    raw_end(1)
    near_send(1, 2)
    gather_relay(0, 0)
    near_share(0, 3)
    near_share(0, 1)
    near_share(0, 2)
    near_end(0)
    for cp in loads:
        cp.wait()
    gather_own(0, 1)
    gate_up(0)
    gather_relay(1, 0)
    near_share(1, 0)
    gather_end(0, 0)
    gate_up(1)
    gather_relay(0, 1)
    gather_end(1, 0)
    near_share(1, 3)
    near_share(1, 1)
    gate_up(2)
    gate_rows()
    gather_own(1, 1)
    near_share(1, 2)
    drain(60)
    near_end(1)
    hidden_grad(0)
    input_grad(0, (2,))
    gather_relay(1, 1)
    input_grad(0, (0,))
    gather_end(0, 1)
    hidden_grad(1)
    dx_arrive(0, 2)
    dx_arrive(0, 0)
    input_grad(1, (2,))
    near_return(0)
    input_grad(1, (0,))
    gather_end(1, 1)
    hidden_grad(2)
    gate_sums()
    dx_arrive(1, 2)
    rings[1].far()
    dx_arrive(1, 0)
    rings[1].near()
    near_return(1)
    input_grad(2, (2,))
    rings[1].relay()
    input_grad(2, (0,))
    dx_arrive(2, 2)
    rings[2].far()
    dx_arrive(2, 0)
    rings[2].near()
    gate_back()
    store(dg, dg_out)
    store(du, du_out)
    scatter3(1)
    rings[2].relay()
    near_combine()
    token_ring.far()
    token_ring.near()
    down_piece(0)
    gate_end()
    drain(50)
    scatter3(2)
    token_ring.relay()
    down_piece(1)
    down_piece(2)
    down_piece(3)
    first, second = token_ring.sums()
    for q in FAR_LIST:
        arrive(("r", q), home.at[block(q)], toward(q))
    far_sum = jnp.zeros((TOK, DS), F32)
    for a, b in GROUPS:
        rows = pl.ds(a * CAP, (b - a) * CAP)
        far_sum = far_sum + tn(pick[rows], home[rows])
    gtok_ref[T1] = (far_sum[: TOK // 2] + first).astype(BF16)
    gtok_ref[T2] = (far_sum[TOK // 2 :] + second).astype(BF16)
    for cp in pieces[4:]:
        cp.wait()
    for cp in sent:
        cp.wait_send()
    for cp in stores:
        cp.wait()


def exchange(tokens, grad_out, routes, gates, w_gate, w_up, w_down):
    vmem = pl.BlockSpec(memory_space=pltpu.VMEM)
    hbm = pl.BlockSpec(memory_space=pl.ANY)
    return pl.pallas_call(
        main_kernel,
        out_shape=(
            jax.ShapeDtypeStruct((TOK, DS), BF16),
            jax.ShapeDtypeStruct((TOPK, TOK), F32),
            jax.ShapeDtypeStruct((SLOTS, D), BF16),
            jax.ShapeDtypeStruct((FS, SLOTS), BF16),
            jax.ShapeDtypeStruct((FS, SLOTS), BF16),
            jax.ShapeDtypeStruct((FS, D), BF16),
        ),
        in_specs=[vmem] * 4 + [hbm] * 3,
        out_specs=(vmem, vmem, hbm, hbm, hbm, hbm),
        scratch_shapes=[
            pltpu.VMEM((2, SLOTS, D), BF16),
            pltpu.VMEM((4, 2, TOK, DS), BF16),
            pltpu.VMEM((2, SLOTS, DS), BF16),
            pltpu.VMEM((3, 2, NR, DS), BF16),
            pltpu.VMEM((SLOTS, TOK), BF16),
            pltpu.VMEM((SLOTS, TOK), BF16),
            pltpu.VMEM((FS, D), BF16),
            pltpu.VMEM((FS, D), BF16),
            pltpu.VMEM((FS, D), BF16),
            pltpu.VMEM((NCH, FS, CH), F32),
            pltpu.VMEM((NCH, FS, CH), F32),
            pltpu.VMEM((FS, SLOTS), BF16),
            pltpu.VMEM((FS, SLOTS), BF16),
            pltpu.VMEM((FS, SLOTS), BF16),
            pltpu.VMEM((FS, SLOTS), BF16),
            pltpu.VMEM((2, FS, 2 * DS), BF16),
            pltpu.VMEM((NB, 8, TOK), F32),
            pltpu.VMEM((NB, 8, TOK), F32),
            pltpu.VMEM((8, SLOTS), F32),
            pltpu.VMEM((8, SLOTS), F32),
            pltpu.VMEM((8, NB, TOK), F32),
            pltpu.VMEM((NB, 8, TOK), F32),
            pltpu.VMEM((NB, 8, TOK), F32),
            pltpu.VMEM((4, SLOTS, DS), F32),
            pltpu.VMEM((4, SLOTS, DS), BF16),
            pltpu.VMEM((4, SLOTS, DS), BF16),
            pltpu.VMEM((3, 6, CH // 2, DS), BF16),
            pltpu.VMEM((3, 6, CH // 2, DS), BF16),
            pltpu.VMEM((4, NR, DS), BF16),
            pltpu.VMEM((4, NR, DS), BF16),
            pltpu.VMEM((4, TOK, DS), F32),
            pltpu.VMEM((SLOTS, DS), BF16),
            pltpu.VMEM((SLOTS, DS), BF16),
            pltpu.SemaphoreType.DMA((N_SEMS,)),
            pltpu.SemaphoreType.DMA((N_SEMS,)),
            pltpu.SemaphoreType.DMA((8,)),
            pltpu.SemaphoreType.DMA((24,)),
            pltpu.SemaphoreType.DMA((26,)),
            pltpu.SemaphoreType.DMA((8,)),
        ],
        compiler_params=pltpu.CompilerParams(
            collective_id=0, has_side_effects=True, vmem_limit_bytes=60 << 20
        ),
        cost_estimate=pl.CostEstimate(
            flops=2 * 5 * SLOTS * FS * D, bytes_accessed=25_000_000, transcendentals=SLOTS * FS
        ),
    )(tokens, grad_out, routes.T, gates.T, w_gate, w_up, w_down)


def weight_kernel(
    tok_ref, gate_ref, x_ref, dg_ref, du_ref, down_ref, tok_out, gate_out, og_ref, ou_ref, od_ref
):
    @pl.when(pl.program_id(0) == 0)
    def _():
        tok_out[...] = tok_ref[...]
        gate_out[...] = gate_ref[...]

    og_ref[0] = nn(dg_ref[...], x_ref[...]).astype(BF16)
    ou_ref[0] = nn(du_ref[...], x_ref[...]).astype(BF16)
    od_ref[0] = down_ref[...]


def weight_grads(grad_tokens, grad_gates, x, dg, du, down):
    tile = 768
    whole = pl.BlockSpec((FS, SLOTS), lambda i: (0, 0))
    small = [pl.BlockSpec(a.shape, lambda i: (0, 0)) for a in (grad_tokens, grad_gates)]
    out = pl.BlockSpec((1, FS, tile), lambda i: (0, 0, i))
    shape = jax.ShapeDtypeStruct((1, FS, D), BF16)
    return pl.pallas_call(
        weight_kernel,
        grid=(D // tile,),
        out_shape=(
            jax.ShapeDtypeStruct(grad_tokens.shape, BF16),
            jax.ShapeDtypeStruct(grad_gates.shape, F32),
            shape, shape, shape,
        ),
        in_specs=[
            *small,
            pl.BlockSpec((SLOTS, tile), lambda i: (0, i)),
            whole,
            whole,
            pl.BlockSpec((FS, tile), lambda i: (0, i)),
        ],
        out_specs=(*small, out, out, out),
        compiler_params=pltpu.CompilerParams(vmem_limit_bytes=62 << 20),
        cost_estimate=pl.CostEstimate(
            flops=2 * 2 * SLOTS * FS * D, bytes_accessed=25_000_000, transcendentals=0
        ),
    )(grad_tokens, grad_gates, x, dg, du, down)


def per_device(tokens, grad_out, routes, gate_values, w_gate, w_up, w_down):
    grad_tokens, grad_gates, x, dg, du, down = exchange(
        tokens, grad_out, routes, gate_values, w_gate, w_up, w_down
    )
    grad_tokens, grad_gates, grad_w_gate, grad_w_up, grad_w_down = weight_grads(
        grad_tokens, grad_gates, x, dg, du, down
    )
    return grad_tokens, grad_gates.T, grad_w_gate, grad_w_up, grad_w_down


def solution(mesh):
    return jax.shard_map(
        per_device,
        mesh=mesh,
        in_specs=(
            P("expert", "dp"),
            P("expert", "dp"),
            P("expert", None),
            P("expert", None),
            P("expert", "dp", None),
            P("expert", "dp", None),
            P("expert", "dp", None),
        ),
        out_specs=(
            P("expert", "dp"),
            P("expert", None),
            P("expert", "dp", None),
            P("expert", "dp", None),
            P("expert", "dp", None),
        ),
        check_vma=False,
    )
```
